128 devices in a mesh: lev: 2 (over x_lo), lat: 64 (over y, z, x_hi, core).
Axes of the slice: x: 4 (x_hi: 2, x_lo: 2; x = x_hi * 2 + x_lo), y: 4, z: 4, core: 2. Of those that a mesh axis runs over, the one named last changes fastest.
Arguments:
- tokens: bfloat16 [8, 384, 24, 512], P('lev', 'lat'), may hold values from -6 to 6
- level_ids: int32 [8], P('lev'), may hold values from 0 to 12
- level_table: float32 [13, 512], replicated, may hold values from -6 to 6
- latent_query: bfloat16 [4, 512], replicated, may hold values from -360 to 360
- w_query: bfloat16 [512, 512], replicated, may hold values from -0.25 to 0.25
- w_kv: bfloat16 [512, 1024], replicated, may hold values from -0.25 to 0.25
- w_attn_out: bfloat16 [512, 512], replicated, may hold values from -0.25 to 0.25
- regions: int32 [384, 24, 4], P('lat', 'lev'), may hold values from 0 to 3
- gain_one: float32 [2, 512], replicated, may hold values from 0.25 to 1.75
- gain_two: float32 [2, 512], replicated, may hold values from 0.25 to 1.75
- w_qkv: bfloat16 [2, 512, 1536], P(None, 'lat'), may hold values from -0.25 to 0.25
- w_proj: bfloat16 [2, 512, 512], P(None, 'lat'), may hold values from -0.25 to 0.25
- w_up: bfloat16 [2, 512, 2048], P(None, 'lat'), may hold values from -0.25 to 0.25
- w_down: bfloat16 [2, 2048, 512], P(None, 'lat'), may hold values from -0.125 to 0.125
Outputs:
- grid_out: bfloat16 [384, 24, 4, 512], P('lat', 'lev')
The draws below stay inside these ranges and needn't reach their ends.
Inputs may be any that keep to these rules, and one draw needn't show every extreme that they name: `regions`: within a window of the shifted grid, tokens attend only to tokens of the same region id.
All inputs are finite; a program needn't handle non-finite values.
Results may differ from the reference program's by a relative error of at most 0.018.
Values may be sent and summed in bfloat16 or wider, within the bound.
A program may use at most 64 MiB of HBM per device.

```python
import jax
import jax.numpy as jnp
from jax import lax

D = 512
HEADS = 16
HD = 32
FF = 2048
Q_LAT = 4
PRESSURE = 13
ROWS_DEV = 6
BLOCKS = 2
LEVELS = 8
H = 384
W = 24
N_LAT = 64


def draw_latent_query(key, part):
    base = jnp.clip(jax.random.normal(key, (Q_LAT, D), jnp.float32), -6.0, 6.0)
    return base.astype(jnp.bfloat16)


def plant(array, key, low, largest):
    extent = array.shape
    index_at = [jax.random.randint(jax.random.fold_in(key, axis), (), 0, extent[axis]) for axis in range(len(extent))]
    array = array.at[tuple(index_at)].set(low)
    longest = extent.index(max(extent))
    index_at[longest] = (index_at[longest] + 1) % extent[longest]
    return array.at[tuple(index_at)].set(largest)


def block_levels(rng, extent, pieces, low, largest):
    factor_of = 1.0
    for position, parts in pieces:
        heights = jax.random.uniform(jax.random.fold_in(jax.random.fold_in(rng, 6), position), (parts,), jnp.float32, low / len(pieces), largest / len(pieces))
        factor_of = factor_of * jnp.repeat(jnp.exp(heights), extent[position] // parts).reshape((-1,) + (1,) * (len(extent) - 1 - position))
    return factor_of


def normal_values(key, shape, deviation, reach, pieces=(), kind=jnp.bfloat16):
    values = jax.random.normal(key, shape, jnp.float32) * deviation
    if len(pieces) > 0:
        values = block_levels(key, shape, pieces, -0.22, 0.18) * values
    return jnp.clip(values, min=-reach, max=reach).astype(kind)


def setup_inputs(seed: int = 0) -> dict:
    key_list = jax.random.split(jax.random.key(seed), 15)
    return {
        "tokens": normal_values(key_list[0], (LEVELS, H, W, D), 1.0, 6.0, ((0, 2), (1, 64))),
        "level_ids": plant(jax.random.randint(key_list[1], (LEVELS,), 0, PRESSURE), jax.random.fold_in(key_list[1], 1), 0, PRESSURE - 1).astype(jnp.int32),
        "level_table": normal_values(key_list[2], (PRESSURE, D), 1.0, 6.0, (), jnp.float32),
        "latent_query": draw_latent_query(jax.random.fold_in(key_list[14], 71), 0),
        "w_query": normal_values(key_list[4], (D, D), D ** -0.5, 0.25),
        "w_kv": normal_values(key_list[5], (D, 2 * D), D ** -0.5, 0.25),
        "w_attn_out": normal_values(key_list[6], (D, D), D ** -0.5, 0.25),
        "regions": plant(jax.random.randint(key_list[7], (H, W, Q_LAT), 0, 4), jax.random.fold_in(key_list[7], 1), 0, 3).astype(jnp.int32),
        "gain_one": jnp.clip(1.0 + 0.15 * jax.random.normal(key_list[8], (BLOCKS, D), jnp.float32), 0.25, 1.75),
        "gain_two": jnp.clip(1.0 + 0.15 * jax.random.normal(key_list[9], (BLOCKS, D), jnp.float32), 0.25, 1.75),
        "w_qkv": normal_values(key_list[10], (BLOCKS, D, 3 * D), D ** -0.5, 0.25, ((1, 64),)),
        "w_proj": normal_values(key_list[11], (BLOCKS, D, D), D ** -0.5, 0.25, ((1, 64),)),
        "w_up": normal_values(key_list[12], (BLOCKS, D, FF), D ** -0.5, 0.25, ((1, 64),)),
        "w_down": normal_values(key_list[13], (BLOCKS, FF, D), FF ** -0.5, 0.125, ((1, 64),)),
    }


eps = 1e-05

def layer_norm(flat, gain):
    mean = lax.optimization_barrier(jnp.mean(flat, -1, keepdims=True))
    centred = flat - mean
    var = lax.optimization_barrier(jnp.mean(centred * centred, -1, keepdims=True))
    return centred * lax.rsqrt(var + eps) * gain

def windows(grid):
    rows, cols, levels, width = grid.shape
    grid = grid.reshape(rows // 6, 6, cols // 12, 12, levels // 2, 2, width)
    grid = grid.transpose(0, 2, 4, 1, 3, 5, 6)
    return grid.reshape(-1, 144, width)

def unwindows(tiles, rows, cols, levels):
    width = tiles.shape[-1]
    tiles = tiles.reshape(rows // 6, cols // 12, levels // 2, 6, 12, 2, width)
    tiles = tiles.transpose(0, 3, 1, 4, 2, 5, 6)
    return tiles.reshape(rows, cols, levels, width)

def level_embed(level_ids, level_table):
    kinds = level_table.shape[0]
    onehot = (level_ids[:, None] == jnp.arange(kinds, dtype=jnp.int32)[None, :]).astype(jnp.float32)
    return jnp.dot(onehot, level_table, precision=lax.Precision.HIGHEST)

def swin_block(grid, regions, gain_a, gain_b, w_qkv, w_proj, w_up, w_down, masked):
    rows, cols, levels, width = grid.shape
    flat = grid.reshape(-1, width).astype(jnp.float32)
    normed = layer_norm(flat, gain_a).astype(jnp.bfloat16)
    qkv = jnp.dot(normed, w_qkv, preferred_element_type=jnp.float32).astype(jnp.bfloat16)
    tiles = windows(qkv.reshape(rows, cols, levels, 3 * width)).reshape(-1, 144, 3, HEADS, HD).astype(jnp.float32)
    score = jnp.einsum('nahe,nbhe->nhab', tiles[:, :, 0], tiles[:, :, 1]) * HD ** (-0.5)
    if masked:
        idents = windows(regions[..., None])[..., 0]
        same = idents[:, :, None] == idents[:, None, :]
        score = jnp.where(same[:, None], score, -1000000000.0)
    top = lax.optimization_barrier(jnp.max(score, -1, keepdims=True))
    weight = jnp.exp(score - top)
    weight = (weight / lax.optimization_barrier(jnp.sum(weight, -1, keepdims=True))).astype(jnp.bfloat16)
    context = jnp.einsum('nhab,nbhe->nahe', weight.astype(jnp.float32), tiles[:, :, 2]).astype(jnp.bfloat16)
    context = unwindows(context.reshape(-1, 144, width), rows, cols, levels).reshape(-1, width)
    mixed = (flat + jnp.dot(context, w_proj, preferred_element_type=jnp.float32)).astype(jnp.bfloat16)
    normed_b = layer_norm(mixed.astype(jnp.float32), gain_b).astype(jnp.bfloat16)
    hidden = jax.nn.gelu(jnp.dot(normed_b, w_up, preferred_element_type=jnp.float32)).astype(jnp.bfloat16)
    result = mixed.astype(jnp.float32) + jnp.dot(hidden, w_down, preferred_element_type=jnp.float32)
    return result.astype(jnp.bfloat16).reshape(rows, cols, levels, width)

def reference(tokens, level_ids, level_table, latent_query, w_query, w_kv, w_attn_out, regions, gain_one, gain_two, w_qkv, w_proj, w_up, w_down):
    embed = level_embed(level_ids, level_table)
    queries = jnp.dot(latent_query, w_query, preferred_element_type=jnp.float32).astype(jnp.bfloat16)
    heads_q = queries.reshape(Q_LAT, HEADS, HD).astype(jnp.float32)

    def encode(band):
        start = (band * ROWS_DEV).astype(jnp.int32)
        piece = lax.dynamic_slice_in_dim(tokens, start, ROWS_DEV, 1)
        summed = (piece.astype(jnp.float32) + embed[:, None, None, :]).astype(jnp.bfloat16)
        kv = jnp.dot(summed.reshape(-1, D), w_kv, preferred_element_type=jnp.float32).astype(jnp.bfloat16)
        kv = kv.reshape(LEVELS, ROWS_DEV, W, 2, HEADS, HD).astype(jnp.float32)
        score = jnp.einsum('qhe,lrwhe->rwqhl', heads_q, kv[:, :, :, 0]) * HD ** (-0.5)
        weight = jax.nn.softmax(score, axis=-1)
        attended = jnp.einsum('rwqhl,lrwhe->rwqhe', weight, kv[:, :, :, 1])
        attended = attended.astype(jnp.bfloat16).reshape(-1, D)
        projected = jnp.dot(attended, w_attn_out, preferred_element_type=jnp.float32).reshape(ROWS_DEV, W, Q_LAT, D)
        return (projected + queries.astype(jnp.float32)).astype(jnp.bfloat16)
    latent = lax.map(encode, jnp.arange(N_LAT, dtype=jnp.int32)).reshape(H, W, Q_LAT, D)

    def plain_slab(slab):
        return swin_block(slab, None, gain_one[0], gain_two[0], w_qkv[0], w_proj[0], w_up[0], w_down[0], False)
    plain = lax.map(plain_slab, latent.reshape(H // 6, 6, W, Q_LAT, D)).reshape(H, W, Q_LAT, D)
    rolled = jnp.roll(plain, (-3, -6, -1), (0, 1, 2))

    def shifted_slab(pair):
        return swin_block(pair[0], pair[1], gain_one[1], gain_two[1], w_qkv[1], w_proj[1], w_up[1], w_down[1], True)
    shifted = lax.map(shifted_slab, (rolled.reshape(H // 6, 6, W, Q_LAT, D), regions.reshape(H // 6, 6, W, Q_LAT)))
    shifted = shifted.reshape(H, W, Q_LAT, D)
    return jnp.roll(shifted, (3, 6, 1), (0, 1, 2))
```

```python
import functools

import jax
import jax.numpy as jnp
import numpy as np
from jax import lax
from jax.experimental import pallas as pl
from jax.experimental.pallas import tpu as pltpu
from jax.sharding import PartitionSpec as P

HEADS = 16
HD = 32
Q_LAT = 4
D = 512
PAD = 80
EPS = 1e-05
BF = jnp.bfloat16
F32 = jnp.float32
EXP_SCALE = float(np.log2(np.e) / np.sqrt(HD))


MESH = pl.DeviceIdType.MESH
ORDERS = ((0, 1, 2), (1, 2, 0), (2, 0, 1))


class Place:
    def __init__(self):
        self.lev = lax.axis_index("lev")
        lat = lax.axis_index("lat")
        self.lat = lat
        self.core = lax.rem(lat, 2)
        xh = lax.rem(lat // 2, 2)
        self.pos = (xh * 2 + self.lev, lat // 16, lax.rem(lat // 4, 4))

    def device(self, axis=None, step=0, core=None):
        x, y, z = [lax.rem(p + step, 4) if a == axis else p for a, p in enumerate(self.pos)]
        c = self.core if core is None else core
        return (lax.rem(x, 2), ((y * 4 + z) * 2 + x // 2) * 2 + c)


def region(where, core):
    x, y, z = where
    full = slice(None)
    if x is None:
        xl, xh = full, full
    elif isinstance(x, tuple):
        xl, xh = x[1], full
    else:
        xl, xh = lax.rem(x, 2), x // 2

    def line(v):
        if v is None:
            return full
        if isinstance(v, tuple):
            return pl.ds(2 * v[1], 2)
        return v

    return (xl, line(y), line(z), xh, core)


class Gather:
    def __init__(self, place, bufs, send, recv):
        self.place, self.bufs, self.send, self.recv = place, bufs, send, recv

    def copy(self, b, p, slot, where, core, device):
        at = self.bufs[p].at[(b,) + region(where, core)]
        return pltpu.make_async_remote_copy(
            src_ref=at,
            dst_ref=at,
            send_sem=self.send.at[b, p, slot],
            recv_sem=self.recv.at[b, p, slot],
            device_id=device,
            device_id_type=MESH,
        )

    def where(self, p, phase, step, half=None):
        order = ORDERS[p]
        place = [None, None, None]
        for k, axis in enumerate(order):
            if k == phase:
                place[axis] = lax.rem(self.place.pos[axis] + step + 4, 4)
            elif k > phase:
                place[axis] = self.place.pos[axis]
            elif k == 0 and half is not None:
                place[axis] = ("half", half)
        return place

    def going(self, b, p, slot):
        pl_ = self.place
        c = pl_.core
        if slot < 3:
            return self.copy(b, p, slot, self.where(p, 0, 0), c, pl_.device(ORDERS[p][0], (1, 3, 2)[slot]))
        if slot < 11:
            phase, k = 1 + (slot - 3) // 4, (slot - 3) % 4
            step, half, to = ((0, None, 1), (0, None, 3), (-1, 0, 1), (1, 1, 3))[k]
            return self.copy(b, p, slot, self.where(p, phase, step, half), c, pl_.device(ORDERS[p][phase], to))
        step = (0, -1, 1, 2)[slot - 11]
        return self.copy(b, p, slot, self.where(p, 2, step), c, pl_.device(core=1 - c))

    def coming(self, b, p, slot):
        pl_ = self.place
        c = pl_.core
        if slot < 3:
            step = (-1, 1, 2)[slot]
            return self.copy(b, p, slot, self.where(p, 0, step), c, pl_.device(ORDERS[p][0], (3, 1, 2)[slot]))
        if slot < 11:
            phase, k = 1 + (slot - 3) // 4, (slot - 3) % 4
            step, half, to = ((-1, None, 3), (1, None, 1), (2, 0, 3), (2, 1, 1))[k]
            return self.copy(b, p, slot, self.where(p, phase, step, half), c, pl_.device(ORDERS[p][phase], to))
        step = (0, -1, 1, 2)[slot - 11]
        return self.copy(b, p, slot, self.where(p, 2, step), 1 - c, pl_.device(core=1 - c))

    STAGES = (
        ((), (0, 1, 2)),
        ((0, 1, 2), (3, 4)),
        ((3, 4), (5, 6)),
        ((5, 6), (7, 8, 11)),
        ((7, 8), (9, 10, 12, 13)),
        ((9, 10), (14,)),
    )

    def stage(self, b, k, parts=(0, 1, 2)):
        waits, sends = self.STAGES[k]
        for p in parts:
            for slot in waits:
                self.coming(b, p, slot).wait_recv()
            for slot in sends:
                self.going(b, p, slot).start()

    def finish(self, b, parts=(0, 1, 2)):
        for p in parts:
            for slot in (11, 12, 13, 14):
                self.coming(b, p, slot).wait_recv()

    def drain(self, b, parts=(0, 1, 2)):
        for p in parts:
            for slot in range(15):
                self.going(b, p, slot).wait_send()


def greet(place, more):
    barrier = pltpu.get_barrier_semaphore()
    peers = [place.device(axis, step) for axis in range(3) for step in (1, 2, 3)]
    peers.append(place.device(core=1 - place.core))
    peers += more
    for peer in peers:
        pl.semaphore_signal(barrier, inc=1, device_id=peer, device_id_type=MESH)
    return barrier, len(peers)


def dot(a, b, dims=((1,), (0,))):
    return lax.dot_general(a, b, (dims, ((), ())), preferred_element_type=F32)


def layer_norm(flat, gain):
    mean = jnp.mean(flat, -1, keepdims=True)
    centred = flat - mean
    var = jnp.mean(centred * centred, -1, keepdims=True)
    return (centred * lax.rsqrt(var + EPS) * gain).astype(BF)


def gelu(x):
    inner = x * (0.7978845608028654 + 0.035677408136300125 * x * x)
    half = 0.5 * x
    return half + half * jnp.tanh(inner)


def one_hot(rows, columns, pairs):
    out = np.zeros((rows, columns), np.float32)
    for i, j in pairs:
        out[i, j] = 1.0
    return out


def cells():
    for k in range(4):
        for r in range(6):
            for c in range(12):
                yield k, r, c


def quarter_row(k, r, c):
    return ((r // 3) * 2 + c // 6) * PAD + k * 18 + (r % 3) * 6 + c % 6


def row_orders():
    halves = np.stack(
        [
            one_hot(
                2 * PAD,
                144,
                [
                    (side * PAD + r * 12 + c, r * 24 + c + 12 * (lev ^ side))
                    for side in range(2)
                    for r in range(6)
                    for c in range(12)
                ],
            )
            for lev in range(2)
        ]
    )
    cut = one_hot(4 * PAD, 288, [(quarter_row(k, r, c), k * 72 + r * 12 + c) for k, r, c in cells()])
    rolled = one_hot(
        288, 4 * PAD, [(k * 72 + r * 12 + c, quarter_row((k + 1) % 4, r, c)) for k, r, c in cells()]
    )
    back = one_hot(
        288, 4 * PAD, [(r * 48 + c * 4 + (k + 1) % 4, quarter_row(k, r, c)) for k, r, c in cells()]
    )
    return [a.astype(BF) for a in (halves, cut, rolled, back)]


def head_spread():
    rows = np.arange(Q_LAT * HEADS)
    return (np.arange(D)[None, :] // HD == rows[:, None] % HEADS).astype(BF)


def pick_head(shape, j):
    lane = lax.broadcasted_iota(jnp.int32, shape, 1)
    return (lane >= j * HD) & (lane < (j + 1) * HD)


def attention(q, k, v, mask):
    parts = []
    for g in range(4):
        lanes = slice(g * 128, (g + 1) * 128)
        kg, vg, qg = k[:, lanes], v[:, lanes], q[:, lanes]
        heads = [pick_head((144, 128), j) for j in range(4)]
        qs = jnp.concatenate([jnp.where(h, qg, jnp.zeros_like(qg)) for h in heads], 0)
        score = dot(kg, qs, ((1,), (1,)))
        if mask is not None:
            score = jnp.where(mask, score, -1e30)
        top = jnp.max(score, 0, keepdims=True)
        weight = jnp.exp2((score - top) * EXP_SCALE)
        weight = (weight * (1.0 / jnp.sum(weight, 0, keepdims=True))).astype(BF)
        out = dot(weight, vg, ((0,), (0,)))
        ctx = jnp.zeros((144, 128), F32)
        for j, h in enumerate(heads):
            ctx = jnp.where(h, out[j * 144 : (j + 1) * 144], ctx)
        parts.append(ctx.astype(BF))
    return jnp.concatenate(parts, 1)


class Block:
    def __init__(self, b, bufs, gain_one, gain_two):
        self.b, self.bufs = b, bufs
        self.gain_one = gain_one[b : b + 1, :]
        self.gain_two = gain_two[b : b + 1, :]

    def attend(self, x, regions=None):
        b, wa = self.b, self.bufs[0]
        n1 = layer_norm(x, self.gain_one)
        qk = dot(n1, wa[b, 0].reshape(D, 1024)).astype(BF)
        wv = wa[b, 1, :, :, :, :, :, 0:512].reshape(D, D)
        v = dot(n1, wv).astype(BF)
        out = []
        for w in range(2):
            rows = slice(w * 144, (w + 1) * 144)
            mask = None
            if regions is not None:
                kinds = lax.broadcasted_iota(jnp.int32, (8, 144), 0)
                ids = jnp.broadcast_to(regions[w : w + 1, :], (8, 144))
                hot = (kinds == ids).astype(F32).astype(BF)
                same = dot(hot, hot, ((0,), (0,)))
                mask = jnp.concatenate([same] * 4, 1) > 0.5
            out.append(attention(qk[rows, 0:D], qk[rows, D : 2 * D], v[rows], mask))
        return jnp.concatenate(out, 0)

    def mix(self, x, context):
        wp = self.bufs[0][self.b, 1, :, :, :, :, :, 512:1024].reshape(D, D)
        return (x + dot(context, wp)).astype(BF).astype(F32)

    def feed(self, mixed):
        b = self.b
        n2 = layer_norm(mixed, self.gain_two)
        sums = [0.0, 0.0]
        for h in range(2):
            hidden = gelu(dot(n2, self.bufs[1][b, h].reshape(D, 1024))).astype(BF)
            for side in range(2):
                wd = self.bufs[2][b, side, 2 * h : 2 * h + 2].reshape(1024, 256)
                sums[side] = sums[side] + dot(hidden, wd)
        return (mixed + jnp.concatenate(sums, 1)).astype(BF)


def moved(send_buf, recv_buf, sems, slot, peer, quarter):
    return pltpu.make_async_remote_copy(
        src_ref=send_buf.at[quarter],
        dst_ref=recv_buf.at[slot],
        send_sem=sems[0].at[slot],
        recv_sem=sems[1].at[slot],
        device_id=peer,
        device_id_type=MESH,
    )


def kernel(
    level_ids,
    tokens,
    level_table,
    latent_query,
    w_query,
    w_kv,
    w_attn_out,
    regions,
    gain_one,
    gain_two,
    w_qkv,
    w_proj,
    w_up,
    w_down,
    spread,
    halves,
    cut,
    roll_rows,
    back_rows,
    out,
    ba,
    bb,
    bc,
    tok_own,
    tok_send,
    tok_recv,
    hs,
    hr,
    hs2,
    hr2,
    send,
    recv,
    tok_sem,
    hsem,
    hrsem,
    h2sem,
    h2rsem,
):
    place = Place()
    lev, lat = place.lev, place.lat
    partner = (1 - lev, lat)
    ahead, behind = lax.rem(lat + 1, 64), lax.rem(lat + 63, 64)
    barrier, count = greet(place, [(lev, ahead), (lev, behind), (1 - lev, ahead), (1 - lev, behind)])
    bufs = (ba, bb, bc)
    g = Gather(place, bufs, send, recv)
    first = lev == 0
    for blk in range(2):
        at = (blk,) + region(place.pos, place.core)
        qkv = w_qkv[blk]
        proj = w_proj[blk]
        ba[at] = jnp.where(first, qkv[:, 0:1024], jnp.concatenate([qkv[:, 1024:1536], proj], 1))
        up = w_up[blk]
        bb[at] = jnp.where(first, up[:, 0:1024], up[:, 1024:2048])
        down = w_down[blk]
        bc[at] = jnp.where(first, down[:, 0:256], down[:, 256:512])
    select = halves[lev]
    for slot in range(4):
        row = level_table[pl.ds(level_ids[slot], 1), :]
        summed = (tokens[slot].astype(F32).reshape(144, D) + row).astype(BF)
        both = dot(select, summed).astype(BF)
        tok_own[slot] = both[0:PAD]
        tok_send[slot] = both[PAD : 2 * PAD]
    pl.semaphore_wait(barrier, count)

    g.stage(0, 0)
    tok = pltpu.make_async_remote_copy(
        src_ref=tok_send,
        dst_ref=tok_recv,
        send_sem=tok_sem.at[0],
        recv_sem=tok_sem.at[1],
        device_id=partner,
        device_id_type=MESH,
    )
    tok.start()
    g.stage(1, 0)

    queries = dot(latent_query[...], w_query[...]).astype(BF).astype(F32)
    wide_q = jnp.concatenate(
        [jnp.broadcast_to(queries[q : q + 1], (HEADS, D)) for q in range(Q_LAT)], 0
    )
    query_block = (wide_q * spread[...].astype(F32)).astype(BF)

    def keys_values(ref):
        kv = dot(ref[...].astype(F32).reshape(4 * PAD, D).astype(BF), w_kv[...]).astype(BF)
        score = dot(kv[:, 0:D], query_block, ((1,), (1,)))
        return score.reshape(4, PAD, Q_LAT * HEADS), kv[:, D : 2 * D].astype(F32).reshape(4, PAD, D)

    score_own, val_own = keys_values(tok_own)
    g.stage(0, 1)
    g.stage(1, 1)
    g.stage(0, 2)
    g.stage(1, 2)
    tok.wait_recv()
    score_par, val_par = keys_values(tok_recv)
    g.stage(0, 3)
    top = jnp.maximum(jnp.max(score_own, 0), jnp.max(score_par, 0))
    w_own = jnp.exp2((score_own - top) * EXP_SCALE)
    w_par = jnp.exp2((score_par - top) * EXP_SCALE)
    inverse = 1.0 / (jnp.sum(w_own, 0) + jnp.sum(w_par, 0))
    w_own = (w_own * inverse).reshape(4 * PAD, Q_LAT * HEADS).astype(BF)
    w_par = (w_par * inverse).reshape(4 * PAD, Q_LAT * HEADS).astype(BF)
    attended = []
    line = lax.broadcasted_iota(jnp.int32, (Q_LAT * HEADS, D), 0)
    for q in range(Q_LAT):
        mine = (line >= q * HEADS) & (line < (q + 1) * HEADS)
        owner = jnp.where(mine, spread[...], jnp.zeros((Q_LAT * HEADS, D), BF))
        total = jnp.sum(dot(w_own, owner).reshape(4, PAD, D) * val_own, 0)
        total = total + jnp.sum(dot(w_par, owner).reshape(4, PAD, D) * val_par, 0)
        attended.append(total[0:72])
    g.stage(0, 4)
    attended = jnp.concatenate(attended, 0).astype(BF)
    base = jnp.concatenate([jnp.broadcast_to(queries[q : q + 1], (72, D)) for q in range(Q_LAT)], 0)
    x = (dot(attended, w_attn_out[...]) + base).astype(BF).astype(F32)
    g.stage(1, 3)
    g.stage(0, 5)
    g.finish(0)

    block = Block(0, bufs, gain_one, gain_two)
    context = block.attend(x)
    g.stage(1, 4)
    mixed = block.mix(x, context)
    plain = block.feed(mixed)
    g.stage(1, 5)
    quarters = dot(cut[...], plain).astype(BF)
    for n in range(4):
        hs[n] = quarters[n * PAD : (n + 1) * PAD]
    sems = (hsem, hrsem)
    sent = [
        moved(hs, hr, sems, 0, partner, 2),
        moved(hs, hr, sems, 1, (lev, behind), 1),
        moved(hs, hr, sems, 2, (1 - lev, behind), 0),
    ]
    for copy in sent:
        copy.start()
    g.finish(1)
    for copy in sent:
        copy.wait_recv()
    tiles = jnp.concatenate([hs[3], hr[0], hr[1], hr[2]], 0)
    x = dot(roll_rows[...], tiles)

    block = Block(1, bufs, gain_one, gain_two)
    context = block.attend(x, regions)
    mixed = block.mix(x, context)
    shifted = block.feed(mixed)
    quarters = dot(cut[...], shifted).astype(BF)
    for n in range(4):
        hs2[n] = quarters[n * PAD : (n + 1) * PAD]
    sems = (h2sem, h2rsem)
    back = [
        moved(hs2, hr2, sems, 0, partner, 1),
        moved(hs2, hr2, sems, 1, (lev, ahead), 2),
        moved(hs2, hr2, sems, 2, (1 - lev, ahead), 3),
    ]
    for copy in back:
        copy.start()
    for copy in back:
        copy.wait_recv()
    tiles = jnp.concatenate([hr2[2], hr2[1], hr2[0], hs2[0]], 0)
    out[...] = dot(back_rows[...], tiles).astype(BF)

    tok.wait_send()
    g.drain(0)
    g.drain(1)
    for copy in sent + back:
        copy.wait_send()


def local(
    tokens,
    level_ids,
    level_table,
    latent_query,
    w_query,
    w_kv,
    w_attn_out,
    regions,
    gain_one,
    gain_two,
    w_qkv,
    w_proj,
    w_up,
    w_down,
):
    labels = jnp.transpose(regions, (2, 0, 1)).reshape(2, 144)
    vmem = pl.BlockSpec(memory_space=pltpu.VMEM)
    consts = [jnp.asarray(head_spread())] + [jnp.asarray(a) for a in row_orders()]
    buf = pltpu.VMEM
    dma = pltpu.SemaphoreType.DMA
    flat = pl.pallas_call(
        kernel,
        out_shape=jax.ShapeDtypeStruct((288, D), BF),
        in_specs=[pl.BlockSpec(memory_space=pltpu.SMEM)] + [vmem] * 18,
        out_specs=vmem,
        scratch_shapes=[
            buf((2, 2, 4, 4, 2, 2, 8, 1024), BF),
            buf((2, 2, 4, 4, 2, 2, 8, 1024), BF),
            buf((2, 2, 4, 4, 2, 2, 32, 256), BF),
            buf((4, PAD, D), BF),
            buf((4, PAD, D), BF),
            buf((4, PAD, D), BF),
            buf((4, PAD, D), BF),
            buf((3, PAD, D), BF),
            buf((4, PAD, D), BF),
            buf((3, PAD, D), BF),
            dma((2, 3, 15)),
            dma((2, 3, 15)),
            dma((2,)),
            dma((3,)),
            dma((3,)),
            dma((3,)),
            dma((3,)),
        ],
        compiler_params=pltpu.CompilerParams(
            collective_id=0, has_side_effects=True, vmem_limit_bytes=56 << 20
        ),
        name="encode_and_blocks",
    )(
        level_ids,
        tokens,
        level_table,
        latent_query,
        w_query,
        w_kv,
        w_attn_out,
        labels,
        gain_one,
        gain_two,
        w_qkv,
        w_proj,
        w_up,
        w_down,
        *consts,
    )
    return flat.reshape(6, 12, Q_LAT, D)


def solution(mesh):
    in_specs = (
        P("lev", "lat", None, None),
        P("lev"),
        P(),
        P(),
        P(),
        P(),
        P(),
        P("lat", "lev", None),
        P(),
        P(),
        P(None, "lat", None),
        P(None, "lat", None),
        P(None, "lat", None),
        P(None, "lat", None),
    )
    out_specs = P("lat", "lev", None, None)
    return jax.shard_map(local, mesh=mesh, in_specs=in_specs, out_specs=out_specs, check_vma=False)
```

```python
import functools

import jax
import jax.numpy as jnp
import numpy as np
from jax import lax
from jax.experimental import pallas as pl
from jax.experimental.pallas import tpu as pltpu
from jax.sharding import PartitionSpec as P

HEADS = 16
HD = 32
Q_LAT = 4
D = 512
PAD = 80
EPS = 1e-05
BF = jnp.bfloat16
F32 = jnp.float32
EXP_SCALE = float(np.log2(np.e) / np.sqrt(HD))


MESH = pl.DeviceIdType.MESH
ORDERS = ((0, 1, 2), (1, 2, 0), (2, 0, 1))


class Place:
    def __init__(self):
        self.lev = lax.axis_index("lev")
        lat = lax.axis_index("lat")
        self.lat = lat
        self.core = lax.rem(lat, 2)
        xh = lax.rem(lat // 2, 2)
        self.pos = (xh * 2 + self.lev, lat // 16, lax.rem(lat // 4, 4))

    def device(self, axis=None, step=0, core=None):
        x, y, z = [lax.rem(p + step, 4) if a == axis else p for a, p in enumerate(self.pos)]
        c = self.core if core is None else core
        return (lax.rem(x, 2), ((y * 4 + z) * 2 + x // 2) * 2 + c)


def region(where, core):
    x, y, z = where
    full = slice(None)
    if x is None:
        xl, xh = full, full
    elif isinstance(x, tuple):
        xl, xh = full, x[1]
    else:
        xl, xh = lax.rem(x, 2), x // 2

    def line(v):
        if v is None:
            return full
        if isinstance(v, tuple):
            return pl.ds(2 * v[1], 2)
        return v

    return (xl, line(y), line(z), xh, core)


SLOTS = 13
EARLY = slice(0, 256)
LATE = slice(256, 1024)
STEPS = (1, 3, 2)


class Gather:
    def __init__(self, place, bufs, send, recv):
        self.place, self.bufs, self.send, self.recv = place, bufs, send, recv

    def copy(self, p, slot, index, device):
        at = self.bufs[p].at[index]
        return pltpu.make_async_remote_copy(
            src_ref=at,
            dst_ref=at,
            send_sem=self.send.at[p, slot],
            recv_sem=self.recv.at[p, slot],
            device_id=device,
            device_id_type=MESH,
        )

    def index(self, p, block, phase, step, core, columns, half=None):
        order = ORDERS[p]
        where = [None, None, None]
        for k, axis in enumerate(order):
            if k == phase:
                if isinstance(step, tuple):
                    own = self.place.pos[axis] // 2
                    where[axis] = ("pair", own if step[1] == 0 else 1 - own)
                elif step is not None:
                    where[axis] = lax.rem(self.place.pos[axis] + step, 4)
            elif k > phase:
                where[axis] = self.place.pos[axis]
            elif k == 0 and half is not None:
                where[axis] = ("pair", half)
        at = region(where, core)
        return (slice(None) if block is None else block,) + at + (slice(None), columns)

    def link(self, p, b, slot, coming):
        c = self.place.core
        full = slice(None)
        if b is None:
            phase, at = 0, slot
        elif slot < 3:
            phase, at = 1, 3 + b * SLOTS + slot
        else:
            phase, at = 2, 3 + b * SLOTS + slot
        axis = ORDERS[p][phase]
        if b is None or slot < 6:
            k = slot % 3
            to = STEPS[k]
            columns = EARLY if phase == 2 else full
            step = (4 - to) % 4 if coming else 0
            return self.copy(p, at, self.index(p, b, phase, step, c, columns), self.place.device(axis, to))
        if slot in (7, 8):
            to = STEPS[slot - 7]
            step = (4 - to) if coming else 0
            return self.copy(p, at, self.index(p, b, 2, step, c, LATE), self.place.device(axis, to))
        if slot in (9, 10):
            to = STEPS[slot - 9]
            step = 2 if coming else 4 - to
            return self.copy(p, at, self.index(p, b, 2, step, c, LATE, slot - 9), self.place.device(axis, to))
        c = 1 - c if coming else c
        other = self.place.device(core=1 - self.place.core)
        if slot == 6:
            return self.copy(p, at, self.index(p, b, 2, None, c, EARLY), other)
        return self.copy(p, at, self.index(p, b, 2, ("pair", slot - 11), c, LATE), other)

    def start(self, b, slots):
        for p in range(3):
            for slot in slots:
                self.link(p, b, slot, False).start()

    def wait(self, b, slots):
        for p in range(3):
            for slot in slots:
                self.link(p, b, slot, True).wait_recv()

    def step(self, b, waits, sends):
        for p in range(3):
            for slot in waits:
                self.link(p, b, slot, True).wait_recv()
            for slot in sends:
                self.link(p, b, slot, False).start()

    def drain(self, b, slots):
        for p in range(3):
            for slot in slots:
                self.link(p, b, slot, False).wait_send()


def greet(place, more):
    barrier = pltpu.get_barrier_semaphore()
    peers = [place.device(axis, step) for axis in range(3) for step in (1, 2, 3)]
    peers.append(place.device(core=1 - place.core))
    peers += more
    for peer in peers:
        pl.semaphore_signal(barrier, inc=1, device_id=peer, device_id_type=MESH)
    return barrier, len(peers)


def dot(a, b, dims=((1,), (0,))):
    return lax.dot_general(a, b, (dims, ((), ())), preferred_element_type=F32)


def layer_norm(flat, gain):
    mean = jnp.mean(flat, -1, keepdims=True)
    centred = flat - mean
    var = jnp.mean(centred * centred, -1, keepdims=True)
    return (centred * lax.rsqrt(var + EPS) * gain).astype(BF)


def gelu(x):
    inner = x * (0.7978845608028654 + 0.035677408136300125 * x * x)
    half = 0.5 * x
    return half + half * jnp.tanh(inner)


def one_hot(rows, columns, pairs):
    out = np.zeros((rows, columns), np.float32)
    for i, j in pairs:
        out[i, j] = 1.0
    return out


def cells():
    for k in range(4):
        for r in range(6):
            for c in range(12):
                yield k, r, c


def quarter_row(k, r, c):
    return ((r // 3) * 2 + c // 6) * PAD + k * 18 + (r % 3) * 6 + c % 6


def row_orders():
    halves = np.stack(
        [
            one_hot(
                2 * PAD,
                144,
                [
                    (side * PAD + r * 12 + c, r * 24 + c + 12 * (lev ^ side))
                    for side in range(2)
                    for r in range(6)
                    for c in range(12)
                ],
            )
            for lev in range(2)
        ]
    )
    cut = one_hot(4 * PAD, 288, [(quarter_row(k, r, c), k * 72 + r * 12 + c) for k, r, c in cells()])
    rolled = one_hot(
        288, 4 * PAD, [(k * 72 + r * 12 + c, quarter_row((k + 1) % 4, r, c)) for k, r, c in cells()]
    )
    back = one_hot(
        288, 4 * PAD, [(r * 48 + c * 4 + (k + 1) % 4, quarter_row(k, r, c)) for k, r, c in cells()]
    )
    return [a.astype(BF) for a in (halves, cut, rolled, back)]


def head_spread():
    rows = np.arange(Q_LAT * HEADS)
    return (np.arange(D)[None, :] // HD == rows[:, None] % HEADS).astype(BF)


def pick_head(shape, j):
    lane = lax.broadcasted_iota(jnp.int32, shape, 1)
    return (lane >= j * HD) & (lane < (j + 1) * HD)


def attention(q, k, v, mask):
    parts = []
    for g in range(4):
        lanes = slice(g * 128, (g + 1) * 128)
        kg, vg, qg = k[:, lanes], v[:, lanes], q[:, lanes]
        heads = [pick_head((144, 128), j) for j in range(4)]
        qs = jnp.concatenate([jnp.where(h, qg, jnp.zeros_like(qg)) for h in heads], 0)
        score = dot(kg, qs, ((1,), (1,)))
        if mask is not None:
            score = jnp.where(mask, score, -1e30)
        top = jnp.max(score, 0, keepdims=True)
        weight = jnp.exp2((score - top) * EXP_SCALE)
        weight = (weight * (1.0 / jnp.sum(weight, 0, keepdims=True))).astype(BF)
        out = dot(weight, vg, ((0,), (0,)))
        ctx = jnp.zeros((144, 128), F32)
        for j, h in enumerate(heads):
            ctx = jnp.where(h, out[j * 144 : (j + 1) * 144], ctx)
        parts.append(ctx.astype(BF))
    return jnp.concatenate(parts, 1)


class Block:
    def __init__(self, b, bufs, gain_one, gain_two):
        self.b, self.bufs = b, bufs
        self.gain_one = gain_one[b : b + 1, :]
        self.gain_two = gain_two[b : b + 1, :]

    def tile(self, p, h, first, last):
        return self.bufs[p][self.b, h, :, :, :, :, :, first:last].reshape(D, last - first)

    def attend(self, x, regions=None):
        n1 = layer_norm(x, self.gain_one)
        q, k, v = [
            jnp.concatenate([dot(n1, self.tile(p, h, 0, 256)).astype(BF) for h in range(2)], 1) for p in range(3)
        ]
        out = []
        for w in range(2):
            rows = slice(w * 144, (w + 1) * 144)
            mask = None
            if regions is not None:
                kinds = lax.broadcasted_iota(jnp.int32, (8, 144), 0)
                ids = jnp.broadcast_to(regions[w], (8, 144))
                hot = (kinds == ids).astype(F32).astype(BF)
                same = dot(hot, hot, ((0,), (0,)))
                mask = jnp.concatenate([same] * 4, 1) > 0.5
            out.append(attention(q[rows], k[rows], v[rows], mask))
        return jnp.concatenate(out, 0)

    def mix(self, x, context):
        added = [dot(context, self.tile(1, h, 512, 768)) for h in range(2)]
        return (x + jnp.concatenate(added, 1)).astype(BF).astype(F32)

    def feed(self, mixed):
        b = self.b
        n2 = layer_norm(mixed, self.gain_two)
        sums = [0.0, 0.0]
        for h in range(2):
            up = [dot(n2, self.tile(0, h, 256, 1024)), dot(n2, self.tile(1, h, 256, 512))]
            hidden = jnp.concatenate([gelu(u).astype(BF) for u in up], 1)
            for side in range(2):
                lines = [self.bufs[1][b, side, 2 * h : 2 * h + 2, :, :, :, :, 768:1024]]
                for i in range(1, 4):
                    lines.append(
                        self.bufs[2][b, side, 2 * h : 2 * h + 2, :, :, :, :, 256 * i : 256 * i + 256]
                    )
                wd = jnp.stack([line.reshape(32, 8, 256) for line in lines], 1).reshape(1024, 256)
                sums[side] = sums[side] + dot(hidden, wd)
        return (mixed + jnp.concatenate(sums, 1)).astype(BF)


def moved(send_buf, recv_buf, sems, slot, peer, quarter):
    return pltpu.make_async_remote_copy(
        src_ref=send_buf.at[quarter],
        dst_ref=recv_buf.at[slot],
        send_sem=sems[0].at[slot],
        recv_sem=sems[1].at[slot],
        device_id=peer,
        device_id_type=MESH,
    )


def kernel(
    level_ids,
    tokens,
    level_table,
    latent_query,
    regions,
    gain_one,
    gain_two,
    w_qkv,
    w_proj,
    w_up,
    w_down,
    halves,
    columns,
    w_query_h,
    w_kv_h,
    w_attn_out_h,
    spread_h,
    cut_h,
    roll_rows_h,
    back_rows_h,
    out,
    ba,
    bb,
    bc,
    tok_own,
    tok_send,
    tok_recv,
    hs,
    hr,
    hs2,
    hr2,
    w_query,
    w_kv,
    w_attn_out,
    spread,
    cut,
    roll_rows,
    back_rows,
    send,
    recv,
    tok_sem,
    hsem,
    hrsem,
    h2sem,
    h2rsem,
    load_sem,
):
    place = Place()
    lev, lat = place.lev, place.lat
    partner = (1 - lev, lat)
    ahead, behind = lax.rem(lat + 1, 64), lax.rem(lat + 63, 64)
    barrier, count = greet(place, [(lev, ahead), (lev, behind), (1 - lev, ahead), (1 - lev, behind)])
    pairs = (
        (w_query_h, w_query),
        (w_kv_h, w_kv),
        (spread_h, spread),
        (w_attn_out_h, w_attn_out),
        (cut_h, cut),
        (roll_rows_h, roll_rows),
        (back_rows_h, back_rows),
    )
    loads = [pltpu.make_async_copy(src, dst, load_sem.at[n]) for n, (src, dst) in enumerate(pairs)]
    for load in loads:
        load.start()
    bufs = (ba, bb, bc)
    g = Gather(place, bufs, send, recv)
    first = lev == 0

    def half(array, start, width, apart):
        return jnp.where(first, array[:, start : start + width], array[:, start + apart : start + apart + width])

    for blk in range(2):
        at = (blk,) + region(place.pos, place.core)
        qkv, up, down = w_qkv[blk], w_up[blk], half(w_down[blk], 0, 256, 256)
        lines = [down[8 * i : 8 * i + 8] for i in range(4)]
        ba[at] = jnp.concatenate([half(qkv, 0, 256, 256), half(up, 0, 768, 1024)], 1)
        bb[at] = jnp.concatenate(
            [half(qkv, 512, 256, 256), half(up, 768, 256, 1024), half(w_proj[blk], 0, 256, 256), lines[0]], 1
        )
        bc[at] = jnp.concatenate([half(qkv, 1024, 256, 256)] + lines[1:], 1)
    select = halves[lev]
    for slot in range(4):
        row = level_table[pl.ds(level_ids[slot], 1), :]
        summed = (tokens[slot].astype(F32).reshape(144, D) + row).astype(BF)
        both = dot(select, summed).astype(BF)
        tok_own[slot] = both[0:PAD]
        tok_send[slot] = both[PAD : 2 * PAD]
    pl.semaphore_wait(barrier, count)

    g.start(None, (0, 1, 2))
    toks = [
        pltpu.make_async_remote_copy(
            src_ref=tok_send.at[pl.ds(2 * n, 2)],
            dst_ref=tok_recv.at[pl.ds(2 * n, 2)],
            send_sem=tok_sem.at[2 * n],
            recv_sem=tok_sem.at[2 * n + 1],
            device_id=partner,
            device_id_type=MESH,
        )
        for n in range(2)
    ]
    toks[0].start()

    loads[0].wait()
    loads[1].wait()
    loads[2].wait()
    queries = dot(latent_query[...], w_query[...]).astype(BF).astype(F32)
    wide_q = jnp.concatenate(
        [jnp.broadcast_to(queries[q : q + 1], (HEADS, D)) for q in range(Q_LAT)], 0
    )
    query_block = (wide_q * spread[...].astype(F32)).astype(BF)

    def keys_values(ref):
        kv = dot(ref[...].astype(F32).reshape(4 * PAD, D).astype(BF), w_kv[...]).astype(BF)
        score = dot(kv[:, 0:D], query_block, ((1,), (1,)))
        return score.reshape(4, PAD, Q_LAT * HEADS), kv[:, D : 2 * D].astype(F32).reshape(4, PAD, D)

    g.step(None, (0, 1, 2), ())
    g.start(0, (0, 1, 2))
    toks[1].start()
    g.start(1, (0, 1, 2))
    score_own, val_own = keys_values(tok_own)
    g.step(0, (0, 1, 2), (3, 4, 5))
    g.start(0, (7, 8))
    toks[0].wait_recv()
    toks[1].wait_recv()
    score_par, val_par = keys_values(tok_recv)
    top = jnp.maximum(jnp.max(score_own, 0), jnp.max(score_par, 0))
    w_own = jnp.exp2((score_own - top) * EXP_SCALE)
    w_par = jnp.exp2((score_par - top) * EXP_SCALE)
    inverse = 1.0 / (jnp.sum(w_own, 0) + jnp.sum(w_par, 0))
    w_own = (w_own * inverse).reshape(4 * PAD, Q_LAT * HEADS).astype(BF)
    w_par = (w_par * inverse).reshape(4 * PAD, Q_LAT * HEADS).astype(BF)
    attended = []
    line = lax.broadcasted_iota(jnp.int32, (Q_LAT * HEADS, D), 0)
    for q in range(Q_LAT):
        mine = (line >= q * HEADS) & (line < (q + 1) * HEADS)
        owner = jnp.where(mine, spread[...], jnp.zeros((Q_LAT * HEADS, D), BF))
        total = jnp.sum(dot(w_own, owner).reshape(4, PAD, D) * val_own, 0)
        total = total + jnp.sum(dot(w_par, owner).reshape(4, PAD, D) * val_par, 0)
        attended.append(total[0:72])
    attended = jnp.concatenate(attended, 0).astype(BF)
    base = jnp.concatenate([jnp.broadcast_to(queries[q : q + 1], (72, D)) for q in range(Q_LAT)], 0)
    loads[3].wait()
    x = (dot(attended, w_attn_out[...]) + base).astype(BF).astype(F32)
    g.step(0, (3, 4, 5), (6,))
    g.wait(0, (6,))

    block = Block(0, bufs, gain_one, gain_two)
    context = block.attend(x)
    g.step(0, (7, 8), (9, 10, 11))
    g.step(1, (0, 1, 2), (3, 4, 5))
    g.start(1, (7, 8))
    g.drain(None, (0, 1, 2))
    g.drain(0, (0, 1, 2, 3, 4, 5, 6))
    placed = dot(regions[0].astype(F32).astype(BF), columns[0])
    for r in range(1, 6):
        placed = placed + dot(regions[r].astype(F32).astype(BF), columns[r])
    ids = placed.astype(jnp.int32)
    labels = [jnp.concatenate([ids[2 * w : 2 * w + 1], ids[2 * w + 1 : 2 * w + 2]], 1) for w in range(2)]
    g.step(0, (9, 10), (12,))
    g.wait(0, (11, 12))
    mixed = block.mix(x, context)
    plain = block.feed(mixed)
    loads[4].wait()
    quarters = dot(cut[...], plain).astype(BF)
    for n in range(4):
        hs[n] = quarters[n * PAD : (n + 1) * PAD]
    sems = (hsem, hrsem)
    sent = [
        moved(hs, hr, sems, 0, partner, 2),
        moved(hs, hr, sems, 1, (lev, behind), 1),
        moved(hs, hr, sems, 2, (1 - lev, behind), 0),
    ]
    for copy in sent:
        copy.start()
    g.step(1, (3, 4, 5), (6,))
    g.step(1, (7, 8), (9, 10, 11))
    loads[5].wait()
    for copy in sent:
        copy.wait_recv()
    tiles = jnp.concatenate([hs[3], hr[0], hr[1], hr[2]], 0)
    x = dot(roll_rows[...], tiles)
    g.wait(1, (6,))

    block = Block(1, bufs, gain_one, gain_two)
    context = block.attend(x, labels)
    g.step(1, (9, 10), (12,))
    g.drain(0, (7, 8, 9, 10, 11, 12))
    g.drain(1, (0, 1, 2, 3, 4, 5, 6))
    g.wait(1, (11, 12))
    mixed = block.mix(x, context)
    shifted = block.feed(mixed)
    quarters = dot(cut[...], shifted).astype(BF)
    for n in range(4):
        hs2[n] = quarters[n * PAD : (n + 1) * PAD]
    sems = (h2sem, h2rsem)
    back = [
        moved(hs2, hr2, sems, 0, partner, 1),
        moved(hs2, hr2, sems, 1, (lev, ahead), 2),
        moved(hs2, hr2, sems, 2, (1 - lev, ahead), 3),
    ]
    for copy in back:
        copy.start()
    for tok in toks:
        tok.wait_send()
    g.drain(1, (7, 8, 9, 10, 11, 12))
    loads[6].wait()
    for copy in sent:
        copy.wait_send()
    for copy in back:
        copy.wait_recv()
    tiles = jnp.concatenate([hr2[2], hr2[1], hr2[0], hs2[0]], 0)
    out[...] = dot(back_rows[...], tiles).astype(BF)
    for copy in back:
        copy.wait_send()


def local(
    tokens,
    level_ids,
    level_table,
    latent_query,
    w_query,
    w_kv,
    w_attn_out,
    regions,
    gain_one,
    gain_two,
    w_qkv,
    w_proj,
    w_up,
    w_down,
):
    place_row = np.stack([one_hot(12, 72, [(c, r * 12 + c) for c in range(12)]) for r in range(6)])
    halves, cut, roll_rows, back_rows = [jnp.asarray(a) for a in row_orders()]
    vmem = pl.BlockSpec(memory_space=pltpu.VMEM)
    whole = pl.BlockSpec(memory_space=pl.ANY)
    buf = pltpu.VMEM
    dma = pltpu.SemaphoreType.DMA
    flat = pl.pallas_call(
        kernel,
        out_shape=jax.ShapeDtypeStruct((288, D), BF),
        in_specs=[pl.BlockSpec(memory_space=pltpu.SMEM)] + [vmem] * 12 + [whole] * 7,
        out_specs=vmem,
        scratch_shapes=[buf((2, 2, 4, 4, 2, 2, 8, 1024), BF)] * 3
        + [
            buf((4, PAD, D), BF),
            buf((4, PAD, D), BF),
            buf((4, PAD, D), BF),
            buf((4, PAD, D), BF),
            buf((3, PAD, D), BF),
            buf((4, PAD, D), BF),
            buf((3, PAD, D), BF),
            buf((D, D), BF),
            buf((D, 2 * D), BF),
            buf((D, D), BF),
            buf((Q_LAT * HEADS, D), BF),
            buf((4 * PAD, 288), BF),
            buf((288, 4 * PAD), BF),
            buf((288, 4 * PAD), BF),
            dma((3, 3 + 2 * SLOTS)),
            dma((3, 3 + 2 * SLOTS)),
            dma((4,)),
            dma((3,)),
            dma((3,)),
            dma((3,)),
            dma((3,)),
            dma((7,)),
        ],
        compiler_params=pltpu.CompilerParams(
            collective_id=0, has_side_effects=True, vmem_limit_bytes=56 << 20
        ),
        name="encode_and_blocks",
    )(
        level_ids,
        tokens,
        level_table,
        latent_query,
        jnp.transpose(regions, (0, 2, 1)),
        gain_one,
        gain_two,
        w_qkv,
        w_proj,
        w_up,
        w_down,
        halves,
        jnp.asarray(place_row.astype(BF)),
        w_query,
        w_kv,
        w_attn_out,
        jnp.asarray(head_spread()),
        cut,
        roll_rows,
        back_rows,
    )
    return flat.reshape(6, 12, Q_LAT, D)


def solution(mesh):
    in_specs = (
        P("lev", "lat", None, None),
        P("lev"),
        P(),
        P(),
        P(),
        P(),
        P(),
        P("lat", "lev", None),
        P(),
        P(),
        P(None, "lat", None),
        P(None, "lat", None),
        P(None, "lat", None),
        P(None, "lat", None),
    )
    out_specs = P("lat", "lev", None, None)
    return jax.shard_map(local, mesh=mesh, in_specs=in_specs, out_specs=out_specs, check_vma=False)
```

```python
import functools

import jax
import jax.numpy as jnp
import numpy as np
from jax import lax
from jax.experimental import pallas as pl
from jax.experimental.pallas import tpu as pltpu
from jax.sharding import PartitionSpec as P

HEADS = 16
HD = 32
Q_LAT = 4
D = 512
CELLS = 72
TILES = CELLS // 8
EPS = 1e-05
BF = jnp.bfloat16
F32 = jnp.float32
EXP_SCALE = float(np.log2(np.e) / np.sqrt(HD))


MESH = pl.DeviceIdType.MESH
ORDERS = ((0, 1, 2), (1, 2, 0), (2, 0, 1))


class Place:
    def __init__(self):
        self.lev = lax.axis_index("lev")
        lat = lax.axis_index("lat")
        self.lat = lat
        self.core = lax.rem(lat, 2)
        xh = lax.rem(lat // 2, 2)
        self.pos = (xh * 2 + self.lev, lat // 16, lax.rem(lat // 4, 4))

    def device(self, axis=None, step=0, core=None):
        x, y, z = [lax.rem(p + step, 4) if a == axis else p for a, p in enumerate(self.pos)]
        c = self.core if core is None else core
        return (lax.rem(x, 2), ((y * 4 + z) * 2 + x // 2) * 2 + c)


def region(where, core):
    x, y, z = where
    full = slice(None)
    if x is None:
        xl, xh = full, full
    elif isinstance(x, tuple):
        xl, xh = full, x[1]
    else:
        xl, xh = lax.rem(x, 2), x // 2

    def line(v):
        if v is None:
            return full
        if isinstance(v, tuple):
            return pl.ds(2 * v[1], 2)
        return v

    return (xl, line(y), line(z), xh, core)


SLOTS = 15
EARLY = 256
WIDTHS = (1152, 768, 1152)
STEPS = (1, 3, 2)


class Gather:
    def __init__(self, place, bufs, send, recv):
        self.place, self.bufs, self.send, self.recv = place, bufs, send, recv

    def copy(self, p, slot, index, device):
        at = self.bufs[p].at[index]
        return pltpu.make_async_remote_copy(
            src_ref=at,
            dst_ref=at,
            send_sem=self.send.at[p, slot],
            recv_sem=self.recv.at[p, slot],
            device_id=device,
            device_id_type=MESH,
        )

    def index(self, p, block, phase, step, core, columns, half=None):
        order = ORDERS[p]
        where = [None, None, None]
        for k, axis in enumerate(order):
            if k == phase:
                if isinstance(step, tuple):
                    own = self.place.pos[axis] // 2
                    where[axis] = ("pair", own if step[1] == 0 else 1 - own)
                elif step is not None:
                    where[axis] = lax.rem(self.place.pos[axis] + step, 4)
            elif k > phase:
                where[axis] = self.place.pos[axis]
            elif k == 0 and half is not None:
                where[axis] = ("pair", half)
        at = region(where, core)
        return (slice(None) if block is None else block,) + at + (slice(None), columns)

    def link(self, p, b, slot, coming):
        c = self.place.core
        full, early, late = slice(None), slice(0, EARLY), slice(EARLY, WIDTHS[p])
        if b is None:
            phase, at = 0, slot
        elif slot < 3:
            phase, at = 1, 3 + b * SLOTS + slot
        else:
            phase, at = 2, 3 + b * SLOTS + slot
        axis = ORDERS[p][phase]
        if b is None or slot < 6:
            k = slot % 3
            to = STEPS[k]
            columns = early if phase == 2 else full
            step = (4 - to) % 4 if coming else 0
            return self.copy(p, at, self.index(p, b, phase, step, c, columns), self.place.device(axis, to))
        if slot in (7, 8, 9, 10):
            way, later = (slot - 7) // 2, (slot - 7) % 2
            to = STEPS[way]
            step = (4 - to) if coming else 0
            return self.copy(p, at, self.index(p, b, 2, step, c, late, way ^ later), self.place.device(axis, to))
        if slot in (11, 12):
            to = STEPS[slot - 11]
            step = 2 if coming else 4 - to
            return self.copy(p, at, self.index(p, b, 2, step, c, late, slot - 11), self.place.device(axis, to))
        c = 1 - c if coming else c
        other = self.place.device(core=1 - self.place.core)
        if slot == 6:
            return self.copy(p, at, self.index(p, b, 2, None, c, early), other)
        return self.copy(p, at, self.index(p, b, 2, ("pair", slot - 13), c, late), other)

    def start(self, b, slots):
        for slot in slots:
            for p in range(3):
                self.link(p, b, slot, False).start()

    def wait(self, b, slots):
        for p in range(3):
            for slot in slots:
                self.link(p, b, slot, True).wait_recv()

    def step(self, b, waits, sends):
        for p in range(3):
            for slot in waits:
                self.link(p, b, slot, True).wait_recv()
            for slot in sends:
                self.link(p, b, slot, False).start()

    def drain(self, b, slots):
        for p in range(3):
            for slot in slots:
                self.link(p, b, slot, False).wait_send()


def greet(place, more):
    barrier = pltpu.get_barrier_semaphore()
    peers = [place.device(axis, step) for axis in range(3) for step in (1, 2, 3)]
    peers.append(place.device(core=1 - place.core))
    peers += more
    for peer in peers:
        pl.semaphore_signal(barrier, inc=1, device_id=peer, device_id_type=MESH)
    return barrier, len(peers)


def dot(a, b, dims=((1,), (0,))):
    return lax.dot_general(a, b, (dims, ((), ())), preferred_element_type=F32)


def layer_norm(flat, gain):
    mean = jnp.mean(flat, -1, keepdims=True)
    centred = flat - mean
    var = jnp.mean(centred * centred, -1, keepdims=True)
    return (centred * lax.rsqrt(var + EPS) * gain).astype(BF)


def gelu(x):
    inner = x * (0.7978845608028654 + 0.035677408136300125 * x * x)
    half = 0.5 * x
    return half + half * jnp.tanh(inner)


def one_hot(rows, columns, pairs):
    out = np.zeros((rows, columns), np.float32)
    for i, j in pairs:
        out[i, j] = 1.0
    return out


def cells():
    for k in range(4):
        for r in range(6):
            for c in range(12):
                yield k, r, c


def quarter_row(k, r, c):
    return ((r // 3) * 2 + c // 6) * CELLS + k * 18 + (r % 3) * 6 + c % 6


def row_orders():
    halves = np.stack(
        [
            one_hot(
                2 * CELLS,
                144,
                [
                    (side * CELLS + r * 12 + c, r * 24 + c + 12 * (lev ^ side))
                    for side in range(2)
                    for r in range(6)
                    for c in range(12)
                ],
            )
            for lev in range(2)
        ]
    )
    cut = one_hot(4 * CELLS, 288, [(quarter_row(k, r, c), k * 72 + r * 12 + c) for k, r, c in cells()])
    rolled = one_hot(
        288, 4 * CELLS, [(k * 72 + r * 12 + c, quarter_row((k + 1) % 4, r, c)) for k, r, c in cells()]
    )
    back = one_hot(
        288, 4 * CELLS, [(r * 48 + c * 4 + (k + 1) % 4, quarter_row(k, r, c)) for k, r, c in cells()]
    )
    return [a.astype(BF) for a in (halves, cut, rolled, back)]


def head_spread():
    rows = np.arange(Q_LAT * HEADS)
    return (np.arange(D)[None, :] // HD == rows[:, None] % HEADS).astype(BF)


def pick_head(shape, j):
    lane = lax.broadcasted_iota(jnp.int32, shape, 1)
    return (lane >= j * HD) & (lane < (j + 1) * HD)


def attention(q, k, v, mask):
    parts = []
    for g in range(4):
        lanes = slice(g * 128, (g + 1) * 128)
        kg, vg, qg = k[:, lanes], v[:, lanes], q[:, lanes]
        heads = [pick_head((144, 128), j) for j in range(4)]
        qs = jnp.concatenate([jnp.where(h, qg, jnp.zeros_like(qg)) for h in heads], 0)
        score = dot(kg, qs, ((1,), (1,)))
        if mask is not None:
            score = jnp.where(mask, score, -1e30)
        top = jnp.max(score, 0, keepdims=True)
        weight = jnp.exp2((score - top) * EXP_SCALE)
        weight = (weight * (1.0 / jnp.sum(weight, 0, keepdims=True))).astype(BF)
        out = dot(weight, vg, ((0,), (0,)))
        ctx = jnp.zeros((144, 128), F32)
        for j, h in enumerate(heads):
            ctx = jnp.where(h, out[j * 144 : (j + 1) * 144], ctx)
        parts.append(ctx.astype(BF))
    return jnp.concatenate(parts, 1)


class Block:
    def __init__(self, b, bufs, gain_one, gain_two):
        self.b, self.bufs = b, bufs
        self.gain_one = gain_one[b : b + 1, :]
        self.gain_two = gain_two[b : b + 1, :]

    def tile(self, p, h, first, last):
        return self.bufs[p][self.b, h, :, :, :, :, :, first:last].reshape(D, last - first)

    def qkv(self, x):
        n1 = layer_norm(x, self.gain_one)
        return [
            jnp.concatenate([dot(n1, self.tile(p, h, 0, 256)).astype(BF) for h in range(2)], 1) for p in range(3)
        ]

    def window(self, qkv, w, regions=None):
        q, k, v = [part[w * 144 : (w + 1) * 144] for part in qkv]
        mask = None
        if regions is not None:
            kinds = lax.broadcasted_iota(jnp.int32, (8, 144), 0)
            ids = jnp.broadcast_to(regions[w], (8, 144))
            hot = (kinds == ids).astype(F32).astype(BF)
            same = dot(hot, hot, ((0,), (0,)))
            mask = jnp.concatenate([same] * 4, 1) > 0.5
        return attention(q, k, v, mask)

    def mix(self, x, context):
        added = [dot(context, self.tile(1, h, 512, 768)) for h in range(2)]
        return (x + jnp.concatenate(added, 1)).astype(BF).astype(F32)

    def feed(self, mixed):
        b = self.b
        n2 = layer_norm(mixed, self.gain_two)
        sums = [0.0, 0.0]
        for h in range(2):
            up = [dot(n2, self.tile(0, h, 256, 1024)), dot(n2, self.tile(1, h, 256, 512))]
            hidden = jnp.concatenate([gelu(u).astype(BF) for u in up], 1)
            for side in range(2):

                def line(p, first, width):
                    part = self.bufs[p][b, side, 2 * h : 2 * h + 2, :, :, :, :, first : first + width]
                    return part.reshape(32, 8, width)

                lines = [jnp.concatenate([line(0, 1024, 128), line(2, 1024, 128)], 2)]
                lines += [line(2, 256 * i, 256) for i in range(1, 4)]
                wd = jnp.stack(lines, 1).reshape(1024, 256)
                sums[side] = sums[side] + dot(hidden, wd)
        return (mixed + jnp.concatenate(sums, 1)).astype(BF)


def moved(send_buf, recv_buf, sems, slot, peer, quarter):
    return pltpu.make_async_remote_copy(
        src_ref=send_buf.at[quarter],
        dst_ref=recv_buf.at[slot],
        send_sem=sems[0].at[slot],
        recv_sem=sems[1].at[slot],
        device_id=peer,
        device_id_type=MESH,
    )


def kernel(
    level_ids,
    level_table_h,
    latent_query_h,
    regions_h,
    gain_one_h,
    gain_two_h,
    tokens_h,
    halves_h,
    w_qkv_h,
    w_proj_h,
    w_up_h,
    w_down_h,
    w_query_h,
    w_kv_h,
    spread_h,
    w_attn_out_h,
    columns_h,
    cut_h,
    roll_rows_h,
    back_rows_h,
    out,
    level_table,
    latent_query,
    regions,
    gain_one,
    gain_two,
    tokens,
    halves,
    w_qkv,
    w_proj,
    w_up,
    w_down,
    w_query,
    w_kv,
    spread,
    w_attn_out,
    columns,
    cut,
    roll_rows,
    back_rows,
    ba,
    bb,
    bc,
    tok_own,
    tok_send,
    tok_recv,
    hs,
    hr,
    hs2,
    hr2,
    send,
    recv,
    tok_sem,
    hsem,
    hrsem,
    h2sem,
    h2rsem,
    load_sem,
):
    place = Place()
    lev, lat = place.lev, place.lat
    partner = (1 - lev, lat)
    ahead, behind = lax.rem(lat + 1, 64), lax.rem(lat + 63, 64)
    barrier, count = greet(place, [(lev, ahead), (lev, behind), (1 - lev, ahead), (1 - lev, behind)])
    pairs = (
        (w_qkv_h, w_qkv),
        (w_proj_h, w_proj),
        (w_up_h, w_up),
        (w_down_h, w_down),
        (level_table_h, level_table),
        (tokens_h, tokens),
        (halves_h, halves),
        (latent_query_h, latent_query),
        (w_query_h, w_query),
        (spread_h, spread),
        (w_kv_h, w_kv),
        (w_attn_out_h, w_attn_out),
        (gain_one_h, gain_one),
        (gain_two_h, gain_two),
        (regions_h, regions),
        (columns_h, columns),
        (cut_h, cut),
        (roll_rows_h, roll_rows),
        (back_rows_h, back_rows),
    )
    loads = [pltpu.make_async_copy(src, dst, load_sem.at[n]) for n, (src, dst) in enumerate(pairs)]
    for load in loads:
        load.start()

    def loaded(first, last):
        for load in loads[first:last]:
            load.wait()

    bufs = (ba, bb, bc)
    g = Gather(place, bufs, send, recv)
    first = lev == 0

    def half(array, start, width, apart):
        return jnp.where(first, array[:, start : start + width], array[:, start + apart : start + apart + width])

    loaded(0, 4)
    for blk in range(2):
        at = (blk,) + region(place.pos, place.core)
        qkv, up, down = w_qkv[blk], w_up[blk], half(w_down[blk], 0, 256, 256)
        lines = [down[8 * i : 8 * i + 8] for i in range(4)]
        ba[at] = jnp.concatenate([half(qkv, 0, 256, 256), half(up, 0, 768, 1024), lines[0][:, 0:128]], 1)
        bb[at] = jnp.concatenate(
            [half(qkv, 512, 256, 256), half(up, 768, 256, 1024), half(w_proj[blk], 0, 256, 256)], 1
        )
        bc[at] = jnp.concatenate([half(qkv, 1024, 256, 256)] + lines[1:] + [lines[0][:, 128:256]], 1)
    loaded(4, 7)
    select = halves[lev]
    for slot in range(4):
        row = level_table[pl.ds(level_ids[slot], 1), :]
        summed = (tokens[slot].astype(F32).reshape(144, D) + row).astype(BF)
        both = dot(select, summed)
        tok_own[slot] = both[0:CELLS].reshape(TILES, 8, D).astype(BF)
        tok_send[slot] = both[CELLS : 2 * CELLS].reshape(TILES, 8, D).astype(BF)
    pl.semaphore_wait(barrier, count)

    g.start(None, (0, 1, 2))
    toks = [
        pltpu.make_async_remote_copy(
            src_ref=tok_send.at[pl.ds(2 * n, 2)],
            dst_ref=tok_recv.at[pl.ds(2 * n, 2)],
            send_sem=tok_sem.at[2 * n],
            recv_sem=tok_sem.at[2 * n + 1],
            device_id=partner,
            device_id_type=MESH,
        )
        for n in range(2)
    ]
    toks[0].start()

    loaded(7, 11)
    queries = dot(latent_query[...], w_query[...]).astype(BF).astype(F32)
    wide_q = jnp.concatenate(
        [jnp.broadcast_to(queries[q : q + 1], (HEADS, D)) for q in range(Q_LAT)], 0
    )
    query_block = (wide_q * spread[...].astype(F32)).astype(BF)

    def keys_values(ref):
        kv = dot(ref[...].reshape(4 * CELLS, D), w_kv[...]).astype(BF)
        score = dot(kv[:, 0:D], query_block, ((1,), (1,)))
        return score.reshape(4, CELLS, Q_LAT * HEADS), kv[:, D : 2 * D].astype(F32).reshape(4, CELLS, D)

    g.step(None, (0, 1, 2), ())
    g.start(0, (0, 1, 2))
    toks[1].start()
    g.start(1, (0, 1, 2))
    score_own, val_own = keys_values(tok_own)
    g.step(0, (0, 1, 2), (3, 4, 5))
    g.start(0, (7, 9, 8, 10))
    toks[0].wait_recv()
    toks[1].wait_recv()
    score_par, val_par = keys_values(tok_recv)
    top = jnp.maximum(jnp.max(score_own, 0), jnp.max(score_par, 0))
    w_own = jnp.exp2((score_own - top) * EXP_SCALE)
    w_par = jnp.exp2((score_par - top) * EXP_SCALE)
    inverse = 1.0 / (jnp.sum(w_own, 0) + jnp.sum(w_par, 0))
    w_own = (w_own * inverse).reshape(4 * CELLS, Q_LAT * HEADS).astype(BF)
    w_par = (w_par * inverse).reshape(4 * CELLS, Q_LAT * HEADS).astype(BF)
    attended = []
    line = lax.broadcasted_iota(jnp.int32, (Q_LAT * HEADS, D), 0)
    for q in range(Q_LAT):
        mine = (line >= q * HEADS) & (line < (q + 1) * HEADS)
        owner = jnp.where(mine, spread[...], jnp.zeros((Q_LAT * HEADS, D), BF))
        total = jnp.sum(dot(w_own, owner).reshape(4, CELLS, D) * val_own, 0)
        total = total + jnp.sum(dot(w_par, owner).reshape(4, CELLS, D) * val_par, 0)
        attended.append(total)
    attended = jnp.concatenate(attended, 0).astype(BF)
    base = jnp.concatenate([jnp.broadcast_to(queries[q : q + 1], (CELLS, D)) for q in range(Q_LAT)], 0)
    loaded(11, 16)
    x = (dot(attended, w_attn_out[...]) + base).astype(BF).astype(F32)
    g.step(0, (3, 4, 5), (6,))
    g.wait(0, (6,))

    block = Block(0, bufs, gain_one, gain_two)
    qkv = block.qkv(x)
    g.step(0, (7, 9), (11, 12))
    g.step(1, (0, 1, 2), (3, 4, 5))
    g.start(1, (7, 9, 8, 10))
    context = [block.window(qkv, 0)]
    g.step(0, (8, 10), (13,))
    context.append(block.window(qkv, 1))
    context = jnp.concatenate(context, 0)
    g.step(0, (11, 12), (14,))
    g.drain(None, (0, 1, 2))
    g.drain(0, (0, 1, 2, 3, 4, 5, 6))
    placed = dot(regions[0].astype(F32).astype(BF), columns[0])
    for r in range(1, 6):
        placed = placed + dot(regions[r].astype(F32).astype(BF), columns[r])
    ids = placed.astype(jnp.int32)
    labels = [jnp.concatenate([ids[2 * w : 2 * w + 1], ids[2 * w + 1 : 2 * w + 2]], 1) for w in range(2)]
    loaded(16, 19)
    g.wait(0, (13, 14))
    mixed = block.mix(x, context)
    plain = block.feed(mixed)
    hs[...] = dot(cut[...], plain).reshape(4, TILES, 8, D).astype(BF)
    sems = (hsem, hrsem)
    sent = [
        moved(hs, hr, sems, 1, (lev, behind), 1),
        moved(hs, hr, sems, 0, partner, 2),
        moved(hs, hr, sems, 2, (1 - lev, behind), 0),
    ]
    for copy in sent:
        copy.start()
    g.step(1, (3, 4, 5), (6,))
    g.step(1, (7, 9), (11, 12))
    g.step(1, (8, 10), (13,))
    for copy in sent:
        copy.wait_recv()
    tiles = jnp.concatenate([part.reshape(CELLS, D) for part in (hs[3], hr[0], hr[1], hr[2])], 0)
    x = dot(roll_rows[...], tiles)
    g.wait(1, (6,))

    block = Block(1, bufs, gain_one, gain_two)
    qkv = block.qkv(x)
    context = [block.window(qkv, 0, labels)]
    g.step(1, (11, 12), (14,))
    context.append(block.window(qkv, 1, labels))
    context = jnp.concatenate(context, 0)
    g.wait(1, (13, 14))
    mixed = block.mix(x, context)
    shifted = block.feed(mixed)
    hs2[...] = dot(cut[...], shifted).reshape(4, TILES, 8, D).astype(BF)
    sems = (h2sem, h2rsem)
    back = [
        moved(hs2, hr2, sems, 1, (lev, ahead), 2),
        moved(hs2, hr2, sems, 0, partner, 1),
        moved(hs2, hr2, sems, 2, (1 - lev, ahead), 3),
    ]
    for copy in back:
        copy.start()
    for tok in toks:
        tok.wait_send()
    g.drain(0, (7, 8, 9, 10, 11, 12, 13, 14))
    g.drain(1, range(SLOTS))
    for copy in sent:
        copy.wait_send()
    for copy in back:
        copy.wait_recv()
    tiles = jnp.concatenate([part.reshape(CELLS, D) for part in (hr2[2], hr2[1], hr2[0], hs2[0])], 0)
    out[...] = dot(back_rows[...], tiles).astype(BF)
    for copy in back:
        copy.wait_send()


def local(
    tokens,
    level_ids,
    level_table,
    latent_query,
    w_query,
    w_kv,
    w_attn_out,
    regions,
    gain_one,
    gain_two,
    w_qkv,
    w_proj,
    w_up,
    w_down,
):
    place_row = np.stack([one_hot(12, 72, [(c, r * 12 + c) for c in range(12)]) for r in range(6)])
    halves, cut, roll_rows, back_rows = [jnp.asarray(a) for a in row_orders()]
    operands = (
        level_table,
        latent_query,
        jnp.transpose(regions, (0, 2, 1)),
        gain_one,
        gain_two,
        tokens,
        halves,
        w_qkv,
        w_proj,
        w_up,
        w_down,
        w_query,
        w_kv,
        jnp.asarray(head_spread()),
        w_attn_out,
        jnp.asarray(place_row.astype(BF)),
        cut,
        roll_rows,
        back_rows,
    )
    buf = pltpu.VMEM
    dma = pltpu.SemaphoreType.DMA
    flat = pl.pallas_call(
        kernel,
        out_shape=jax.ShapeDtypeStruct((288, D), BF),
        in_specs=[pl.BlockSpec(memory_space=pltpu.SMEM)]
        + [pl.BlockSpec(memory_space=pl.ANY)] * len(operands),
        out_specs=pl.BlockSpec(memory_space=pltpu.VMEM),
        scratch_shapes=[buf(a.shape, a.dtype) for a in operands]
        + [buf((2, 2, 4, 4, 2, 2, 8, width), BF) for width in WIDTHS]
        + [buf((n, TILES, 8, D), BF) for n in (4, 4, 4, 4, 3, 4, 3)]
        + [
            dma((3, 3 + 2 * SLOTS)),
            dma((3, 3 + 2 * SLOTS)),
            dma((4,)),
            dma((3,)),
            dma((3,)),
            dma((3,)),
            dma((3,)),
            dma((len(operands),)),
        ],
        compiler_params=pltpu.CompilerParams(
            collective_id=0, has_side_effects=True, vmem_limit_bytes=56 << 20
        ),
        name="encode_and_blocks",
    )(level_ids, *operands)
    return flat.reshape(6, 12, Q_LAT, D)


def solution(mesh):
    in_specs = (
        P("lev", "lat", None, None),
        P("lev"),
        P(),
        P(),
        P(),
        P(),
        P(),
        P("lat", "lev", None),
        P(),
        P(),
        P(None, "lat", None),
        P(None, "lat", None),
        P(None, "lat", None),
        P(None, "lat", None),
    )
    out_specs = P("lat", "lev", None, None)
    return jax.shard_map(local, mesh=mesh, in_specs=in_specs, out_specs=out_specs, check_vma=False)
```

```python
import functools

import jax
import jax.numpy as jnp
import numpy as np
from jax import lax
from jax.experimental import pallas as pl
from jax.experimental.pallas import tpu as pltpu
from jax.sharding import PartitionSpec as P

HEADS = 16
HD = 32
Q_LAT = 4
D = 512
CELLS = 72
TILES = CELLS // 8
EPS = 1e-05
BF = jnp.bfloat16
F32 = jnp.float32
EXP_SCALE = float(np.log2(np.e) / np.sqrt(HD))


MESH = pl.DeviceIdType.MESH
ORDERS = ((0, 1, 2), (1, 2, 0), (2, 0, 1))


class Place:
    def __init__(self):
        self.lev = lax.axis_index("lev")
        lat = lax.axis_index("lat")
        self.lat = lat
        self.core = lax.rem(lat, 2)
        xh = lax.rem(lat // 2, 2)
        self.pos = (xh * 2 + self.lev, lat // 16, lax.rem(lat // 4, 4))

    def device(self, axis=None, step=0, core=None):
        x, y, z = [lax.rem(p + step, 4) if a == axis else p for a, p in enumerate(self.pos)]
        c = self.core if core is None else core
        return (lax.rem(x, 2), ((y * 4 + z) * 2 + x // 2) * 2 + c)


def region(where, core):
    x, y, z = where
    full = slice(None)
    if x is None:
        xl, xh = full, full
    elif isinstance(x, tuple):
        xl, xh = full, x[1]
    else:
        xl, xh = lax.rem(x, 2), x // 2

    def line(v):
        if v is None:
            return full
        if isinstance(v, tuple):
            return pl.ds(2 * v[1], 2)
        return v

    return (xl, line(y), line(z), xh, core)


SLOTS = 15
EARLY = 256
WIDTHS = (1152, 768, 1152)
STEPS = (1, 3, 2)


class Gather:
    def __init__(self, place, bufs, send, recv):
        self.place, self.bufs, self.send, self.recv = place, bufs, send, recv

    def copy(self, p, slot, index, device):
        at = self.bufs[p].at[index]
        return pltpu.make_async_remote_copy(
            src_ref=at,
            dst_ref=at,
            send_sem=self.send.at[p, slot],
            recv_sem=self.recv.at[p, slot],
            device_id=device,
            device_id_type=MESH,
        )

    def index(self, p, block, phase, step, core, columns, half=None):
        order = ORDERS[p]
        where = [None, None, None]
        for k, axis in enumerate(order):
            if k == phase:
                if isinstance(step, tuple):
                    own = self.place.pos[axis] // 2
                    where[axis] = ("pair", own if step[1] == 0 else 1 - own)
                elif step is not None:
                    where[axis] = lax.rem(self.place.pos[axis] + step, 4)
            elif k > phase:
                where[axis] = self.place.pos[axis]
            elif k == 0 and half is not None:
                where[axis] = ("pair", half)
        at = region(where, core)
        return (slice(None) if block is None else block,) + at + (slice(None), columns)

    def link(self, p, b, slot, coming):
        c = self.place.core
        full, early, late = slice(None), slice(0, EARLY), slice(EARLY, WIDTHS[p])
        if b is None:
            phase, at = 0, slot
        elif slot < 3:
            phase, at = 1, 3 + b * SLOTS + slot
        else:
            phase, at = 2, 3 + b * SLOTS + slot
        axis = ORDERS[p][phase]
        if b is None or slot < 6:
            k = slot % 3
            to = STEPS[k]
            columns = early if phase == 2 else full
            step = (4 - to) % 4 if coming else 0
            return self.copy(p, at, self.index(p, b, phase, step, c, columns), self.place.device(axis, to))
        if slot in (7, 8, 9, 10):
            way, later = (slot - 7) // 2, (slot - 7) % 2
            to = STEPS[way]
            step = (4 - to) if coming else 0
            return self.copy(p, at, self.index(p, b, 2, step, c, late, way ^ later), self.place.device(axis, to))
        if slot in (11, 12):
            to = STEPS[slot - 11]
            step = 2 if coming else 4 - to
            return self.copy(p, at, self.index(p, b, 2, step, c, late, slot - 11), self.place.device(axis, to))
        c = 1 - c if coming else c
        other = self.place.device(core=1 - self.place.core)
        if slot == 6:
            return self.copy(p, at, self.index(p, b, 2, None, c, early), other)
        return self.copy(p, at, self.index(p, b, 2, ("pair", slot - 13), c, late), other)

    def start(self, b, slots):
        for slot in slots:
            for p in range(3):
                self.link(p, b, slot, False).start()

    def wait(self, b, slots):
        for p in range(3):
            for slot in slots:
                self.link(p, b, slot, True).wait_recv()

    def step(self, b, waits, sends):
        for p in range(3):
            for slot in waits:
                self.link(p, b, slot, True).wait_recv()
            for slot in sends:
                self.link(p, b, slot, False).start()

    def drain(self, b, slots):
        for p in range(3):
            for slot in slots:
                self.link(p, b, slot, False).wait_send()


def greet(place, more):
    barrier = pltpu.get_barrier_semaphore()
    peers = [place.device(axis, step) for axis in range(3) for step in (1, 2, 3)]
    peers.append(place.device(core=1 - place.core))
    peers += more
    for peer in peers:
        pl.semaphore_signal(barrier, inc=1, device_id=peer, device_id_type=MESH)
    return barrier, len(peers)


def dot(a, b, dims=((1,), (0,))):
    return lax.dot_general(a, b, (dims, ((), ())), preferred_element_type=F32)


def layer_norm(flat, gain):
    mean = jnp.mean(flat, -1, keepdims=True)
    centred = flat - mean
    var = jnp.mean(centred * centred, -1, keepdims=True)
    return (centred * lax.rsqrt(var + EPS) * gain).astype(BF)


def gelu(x):
    inner = x * (0.7978845608028654 + 0.035677408136300125 * x * x)
    half = 0.5 * x
    return half + half * jnp.tanh(inner)


def one_hot(rows, columns, pairs):
    out = np.zeros((rows, columns), np.float32)
    for i, j in pairs:
        out[i, j] = 1.0
    return out


def cells():
    for k in range(4):
        for r in range(6):
            for c in range(12):
                yield k, r, c


def quarter_row(k, r, c):
    return ((r // 3) * 2 + c // 6) * CELLS + k * 18 + (r % 3) * 6 + c % 6


def row_orders():
    halves = np.stack(
        [
            one_hot(
                2 * CELLS,
                144,
                [
                    (side * CELLS + r * 12 + c, r * 24 + c + 12 * (lev ^ side))
                    for side in range(2)
                    for r in range(6)
                    for c in range(12)
                ],
            )
            for lev in range(2)
        ]
    )
    cut = one_hot(4 * CELLS, 288, [(quarter_row(k, r, c), k * 72 + r * 12 + c) for k, r, c in cells()])
    rolled = one_hot(
        288, 4 * CELLS, [(k * 72 + r * 12 + c, quarter_row((k + 1) % 4, r, c)) for k, r, c in cells()]
    )
    back = one_hot(
        288, 4 * CELLS, [(r * 48 + c * 4 + (k + 1) % 4, quarter_row(k, r, c)) for k, r, c in cells()]
    )
    return [a.astype(BF) for a in (halves, cut, rolled, back)]


def head_spread():
    rows = np.arange(Q_LAT * HEADS)
    return (np.arange(D)[None, :] // HD == rows[:, None] % HEADS).astype(BF)


def pick_head(shape, j):
    lane = lax.broadcasted_iota(jnp.int32, shape, 1)
    return (lane >= j * HD) & (lane < (j + 1) * HD)


def attention(q, k, v, mask):
    parts = []
    for g in range(4):
        lanes = slice(g * 128, (g + 1) * 128)
        kg, vg, qg = k[:, lanes], v[:, lanes], q[:, lanes]
        heads = [pick_head((144, 128), j) for j in range(4)]
        qs = jnp.concatenate([jnp.where(h, qg, jnp.zeros_like(qg)) for h in heads], 0)
        score = dot(kg, qs, ((1,), (1,)))
        if mask is not None:
            score = jnp.where(mask, score, -1e30)
        top = jnp.max(score, 0, keepdims=True)
        weight = jnp.exp2((score - top) * EXP_SCALE)
        weight = (weight * (1.0 / jnp.sum(weight, 0, keepdims=True))).astype(BF)
        out = dot(weight, vg, ((0,), (0,)))
        ctx = jnp.zeros((144, 128), F32)
        for j, h in enumerate(heads):
            ctx = jnp.where(h, out[j * 144 : (j + 1) * 144], ctx)
        parts.append(ctx.astype(BF))
    return jnp.concatenate(parts, 1)


class Block:
    def __init__(self, b, bufs, gain_one, gain_two):
        self.b, self.bufs = b, bufs
        self.gain_one = gain_one[b : b + 1, :]
        self.gain_two = gain_two[b : b + 1, :]

    def tile(self, p, h, first, last):
        return self.bufs[p][self.b, h, :, :, :, :, :, first:last].reshape(D, last - first)

    def qkv(self, x):
        n1 = layer_norm(x, self.gain_one)
        return [
            jnp.concatenate([dot(n1, self.tile(p, h, 0, 256)).astype(BF) for h in range(2)], 1) for p in range(3)
        ]

    def window(self, qkv, w, regions=None):
        q, k, v = [part[w * 144 : (w + 1) * 144] for part in qkv]
        mask = None
        if regions is not None:
            kinds = lax.broadcasted_iota(jnp.int32, (8, 144), 0)
            ids = jnp.broadcast_to(regions[w], (8, 144))
            hot = (kinds == ids).astype(F32).astype(BF)
            same = dot(hot, hot, ((0,), (0,)))
            mask = jnp.concatenate([same] * 4, 1) > 0.5
        return attention(q, k, v, mask)

    def mix(self, x, context):
        added = [dot(context, self.tile(1, h, 512, 768)) for h in range(2)]
        return (x + jnp.concatenate(added, 1)).astype(BF).astype(F32)

    def feed(self, mixed):
        b = self.b
        n2 = layer_norm(mixed, self.gain_two)
        sums = [0.0, 0.0]
        for h in range(2):
            up = [dot(n2, self.tile(0, h, 256, 1024)), dot(n2, self.tile(1, h, 256, 512))]
            hidden = jnp.concatenate([gelu(u).astype(BF) for u in up], 1)
            for side in range(2):

                def line(p, first, width):
                    part = self.bufs[p][b, side, 2 * h : 2 * h + 2, :, :, :, :, first : first + width]
                    return part.reshape(32, 8, width)

                lines = [jnp.concatenate([line(0, 1024, 128), line(2, 1024, 128)], 2)]
                lines += [line(2, 256 * i, 256) for i in range(1, 4)]
                wd = jnp.stack(lines, 1).reshape(1024, 256)
                sums[side] = sums[side] + dot(hidden, wd)
        return (mixed + jnp.concatenate(sums, 1)).astype(BF)


def moved(send_buf, recv_buf, sems, slot, peer, quarter):
    return pltpu.make_async_remote_copy(
        src_ref=send_buf.at[quarter],
        dst_ref=recv_buf.at[slot],
        send_sem=sems[0].at[slot],
        recv_sem=sems[1].at[slot],
        device_id=peer,
        device_id_type=MESH,
    )


def kernel(
    level_ids,
    level_table_h,
    latent_query_h,
    regions_h,
    gain_one_h,
    gain_two_h,
    tokens_h,
    halves_h,
    w_qkv_h,
    w_proj_h,
    w_up_h,
    w_down_h,
    w_query_h,
    w_kv_h,
    spread_h,
    w_attn_out_h,
    columns_h,
    cut_h,
    roll_rows_h,
    back_rows_h,
    out,
    level_table,
    latent_query,
    regions,
    gain_one,
    gain_two,
    tokens,
    halves,
    w_qkv,
    w_proj,
    w_up,
    w_down,
    w_query,
    w_kv,
    spread,
    w_attn_out,
    columns,
    cut,
    roll_rows,
    back_rows,
    ba,
    bb,
    bc,
    tok_own,
    tok_send,
    tok_recv,
    hs,
    hr,
    hs2,
    hr2,
    send,
    recv,
    tok_sem,
    hsem,
    hrsem,
    h2sem,
    h2rsem,
    load_sem,
):
    place = Place()
    lev, lat = place.lev, place.lat
    partner = (1 - lev, lat)
    ahead, behind = lax.rem(lat + 1, 64), lax.rem(lat + 63, 64)
    barrier, count = greet(place, [(lev, ahead), (lev, behind), (1 - lev, ahead), (1 - lev, behind)])
    pairs = (
        (w_qkv_h, w_qkv),
        (w_proj_h, w_proj),
        (w_up_h, w_up),
        (w_down_h, w_down),
        (level_table_h, level_table),
        (tokens_h, tokens),
        (halves_h, halves),
        (latent_query_h, latent_query),
        (w_query_h, w_query),
        (spread_h, spread),
        (w_kv_h, w_kv),
        (w_attn_out_h, w_attn_out),
        (gain_one_h, gain_one),
        (gain_two_h, gain_two),
        (regions_h, regions),
        (columns_h, columns),
        (cut_h, cut),
        (roll_rows_h, roll_rows),
        (back_rows_h, back_rows),
    )
    loads = [pltpu.make_async_copy(src, dst, load_sem.at[n]) for n, (src, dst) in enumerate(pairs)]
    for load in loads:
        load.start()

    def loaded(first, last):
        for load in loads[first:last]:
            load.wait()

    bufs = (ba, bb, bc)
    g = Gather(place, bufs, send, recv)
    first = lev == 0

    def half(array, start, width, apart):
        return jnp.where(first, array[:, start : start + width], array[:, start + apart : start + apart + width])

    loaded(0, 4)
    for blk in range(2):
        at = (blk,) + region(place.pos, place.core)
        qkv, up, down = w_qkv[blk], w_up[blk], half(w_down[blk], 0, 256, 256)
        lines = [down[8 * i : 8 * i + 8] for i in range(4)]
        ba[at] = jnp.concatenate([half(qkv, 0, 256, 256), half(up, 0, 768, 1024), lines[0][:, 0:128]], 1)
        bb[at] = jnp.concatenate(
            [half(qkv, 512, 256, 256), half(up, 768, 256, 1024), half(w_proj[blk], 0, 256, 256)], 1
        )
        bc[at] = jnp.concatenate([half(qkv, 1024, 256, 256)] + lines[1:] + [lines[0][:, 128:256]], 1)
    pl.semaphore_wait(barrier, count)

    g.start(None, (0, 1, 2))
    loaded(4, 7)
    select = halves[lev]
    for slot in range(4):
        row = level_table[pl.ds(level_ids[slot], 1), :]
        summed = (tokens[slot].astype(F32).reshape(144, D) + row).astype(BF)
        both = dot(select, summed)
        tok_own[slot] = both[0:CELLS].reshape(TILES, 8, D).astype(BF)
        tok_send[slot] = both[CELLS : 2 * CELLS].reshape(TILES, 8, D).astype(BF)
    toks = [
        pltpu.make_async_remote_copy(
            src_ref=tok_send.at[pl.ds(2 * n, 2)],
            dst_ref=tok_recv.at[pl.ds(2 * n, 2)],
            send_sem=tok_sem.at[2 * n],
            recv_sem=tok_sem.at[2 * n + 1],
            device_id=partner,
            device_id_type=MESH,
        )
        for n in range(2)
    ]
    toks[0].start()

    loaded(7, 11)
    queries = dot(latent_query[...], w_query[...]).astype(BF).astype(F32)
    wide_q = jnp.concatenate(
        [jnp.broadcast_to(queries[q : q + 1], (HEADS, D)) for q in range(Q_LAT)], 0
    )
    query_block = (wide_q * spread[...].astype(F32)).astype(BF)

    def keys_values(ref):
        kv = dot(ref[...].reshape(4 * CELLS, D), w_kv[...]).astype(BF)
        score = dot(kv[:, 0:D], query_block, ((1,), (1,)))
        return score.reshape(4, CELLS, Q_LAT * HEADS), kv[:, D : 2 * D].astype(F32).reshape(4, CELLS, D)

    g.step(None, (0, 1, 2), ())
    g.start(0, (0, 1, 2))
    toks[1].start()
    score_own, val_own = keys_values(tok_own)
    g.step(0, (0, 1, 2), (3, 4, 5))
    g.start(0, (7, 9, 8, 10))
    g.start(1, (0, 1, 2))
    toks[0].wait_recv()
    toks[1].wait_recv()
    score_par, val_par = keys_values(tok_recv)
    top = jnp.maximum(jnp.max(score_own, 0), jnp.max(score_par, 0))
    w_own = jnp.exp2((score_own - top) * EXP_SCALE)
    w_par = jnp.exp2((score_par - top) * EXP_SCALE)
    inverse = 1.0 / (jnp.sum(w_own, 0) + jnp.sum(w_par, 0))
    w_own = (w_own * inverse).reshape(4 * CELLS, Q_LAT * HEADS).astype(BF)
    w_par = (w_par * inverse).reshape(4 * CELLS, Q_LAT * HEADS).astype(BF)
    attended = []
    line = lax.broadcasted_iota(jnp.int32, (Q_LAT * HEADS, D), 0)
    for q in range(Q_LAT):
        mine = (line >= q * HEADS) & (line < (q + 1) * HEADS)
        owner = jnp.where(mine, spread[...], jnp.zeros((Q_LAT * HEADS, D), BF))
        total = jnp.sum(dot(w_own, owner).reshape(4, CELLS, D) * val_own, 0)
        total = total + jnp.sum(dot(w_par, owner).reshape(4, CELLS, D) * val_par, 0)
        attended.append(total)
    attended = jnp.concatenate(attended, 0).astype(BF)
    base = jnp.concatenate([jnp.broadcast_to(queries[q : q + 1], (CELLS, D)) for q in range(Q_LAT)], 0)
    loaded(11, 16)
    x = (dot(attended, w_attn_out[...]) + base).astype(BF).astype(F32)
    g.step(0, (3, 4, 5), (6,))
    g.wait(0, (6,))

    block = Block(0, bufs, gain_one, gain_two)
    g.step(0, (7, 9), (11, 12))
    qkv = block.qkv(x)
    context = [block.window(qkv, 0)]
    g.step(0, (8, 10), (13,))
    g.step(1, (0, 1, 2), (3, 4, 5))
    g.start(1, (7, 9, 8, 10))
    context.append(block.window(qkv, 1))
    context = jnp.concatenate(context, 0)
    g.step(0, (11, 12), (14,))
    g.drain(None, (0, 1, 2))
    g.drain(0, (0, 1, 2, 3, 4, 5, 6))
    placed = dot(regions[0].astype(F32).astype(BF), columns[0])
    for r in range(1, 6):
        placed = placed + dot(regions[r].astype(F32).astype(BF), columns[r])
    ids = placed.astype(jnp.int32)
    labels = [jnp.concatenate([ids[2 * w : 2 * w + 1], ids[2 * w + 1 : 2 * w + 2]], 1) for w in range(2)]
    loaded(16, 19)
    g.wait(0, (13, 14))
    mixed = block.mix(x, context)
    plain = block.feed(mixed)
    hs[...] = dot(cut[...], plain).reshape(4, TILES, 8, D).astype(BF)
    sems = (hsem, hrsem)
    sent = [
        moved(hs, hr, sems, 1, (lev, behind), 1),
        moved(hs, hr, sems, 0, partner, 2),
        moved(hs, hr, sems, 2, (1 - lev, behind), 0),
    ]
    for copy in sent:
        copy.start()
    g.step(1, (3, 4, 5), (6,))
    g.step(1, (7, 9), (11, 12))
    g.step(1, (8, 10), (13,))
    for copy in sent:
        copy.wait_recv()
    tiles = jnp.concatenate([part.reshape(CELLS, D) for part in (hs[3], hr[0], hr[1], hr[2])], 0)
    x = dot(roll_rows[...], tiles)
    g.wait(1, (6,))

    block = Block(1, bufs, gain_one, gain_two)
    qkv = block.qkv(x)
    context = [block.window(qkv, 0, labels)]
    g.step(1, (11, 12), (14,))
    context.append(block.window(qkv, 1, labels))
    context = jnp.concatenate(context, 0)
    g.wait(1, (13, 14))
    mixed = block.mix(x, context)
    shifted = block.feed(mixed)
    hs2[...] = dot(cut[...], shifted).reshape(4, TILES, 8, D).astype(BF)
    sems = (h2sem, h2rsem)
    back = [
        moved(hs2, hr2, sems, 1, (lev, ahead), 2),
        moved(hs2, hr2, sems, 0, partner, 1),
        moved(hs2, hr2, sems, 2, (1 - lev, ahead), 3),
    ]
    for copy in back:
        copy.start()
    for tok in toks:
        tok.wait_send()
    g.drain(0, (7, 8, 9, 10, 11, 12, 13, 14))
    g.drain(1, range(SLOTS))
    for copy in sent:
        copy.wait_send()
    for copy in back:
        copy.wait_recv()
    tiles = jnp.concatenate([part.reshape(CELLS, D) for part in (hr2[2], hr2[1], hr2[0], hs2[0])], 0)
    out[...] = dot(back_rows[...], tiles).astype(BF)
    for copy in back:
        copy.wait_send()


def local(
    tokens,
    level_ids,
    level_table,
    latent_query,
    w_query,
    w_kv,
    w_attn_out,
    regions,
    gain_one,
    gain_two,
    w_qkv,
    w_proj,
    w_up,
    w_down,
):
    place_row = np.stack([one_hot(12, 72, [(c, r * 12 + c) for c in range(12)]) for r in range(6)])
    halves, cut, roll_rows, back_rows = [jnp.asarray(a) for a in row_orders()]
    operands = (
        level_table,
        latent_query,
        jnp.transpose(regions, (0, 2, 1)),
        gain_one,
        gain_two,
        tokens,
        halves,
        w_qkv,
        w_proj,
        w_up,
        w_down,
        w_query,
        w_kv,
        jnp.asarray(head_spread()),
        w_attn_out,
        jnp.asarray(place_row.astype(BF)),
        cut,
        roll_rows,
        back_rows,
    )
    buf = pltpu.VMEM
    dma = pltpu.SemaphoreType.DMA
    flat = pl.pallas_call(
        kernel,
        out_shape=jax.ShapeDtypeStruct((288, D), BF),
        in_specs=[pl.BlockSpec(memory_space=pltpu.SMEM)]
        + [pl.BlockSpec(memory_space=pl.ANY)] * len(operands),
        out_specs=pl.BlockSpec(memory_space=pltpu.VMEM),
        scratch_shapes=[buf(a.shape, a.dtype) for a in operands]
        + [buf((2, 2, 4, 4, 2, 2, 8, width), BF) for width in WIDTHS]
        + [buf((n, TILES, 8, D), BF) for n in (4, 4, 4, 4, 3, 4, 3)]
        + [
            dma((3, 3 + 2 * SLOTS)),
            dma((3, 3 + 2 * SLOTS)),
            dma((4,)),
            dma((3,)),
            dma((3,)),
            dma((3,)),
            dma((3,)),
            dma((len(operands),)),
        ],
        compiler_params=pltpu.CompilerParams(
            collective_id=0, has_side_effects=True, vmem_limit_bytes=56 << 20
        ),
        name="encode_and_blocks",
    )(level_ids, *operands)
    return flat.reshape(6, 12, Q_LAT, D)


def solution(mesh):
    in_specs = (
        P("lev", "lat", None, None),
        P("lev"),
        P(),
        P(),
        P(),
        P(),
        P(),
        P("lat", "lev", None),
        P(),
        P(),
        P(None, "lat", None),
        P(None, "lat", None),
        P(None, "lat", None),
        P(None, "lat", None),
    )
    out_specs = P("lat", "lev", None, None)
    return jax.shard_map(local, mesh=mesh, in_specs=in_specs, out_specs=out_specs, check_vma=False)
```

```python
import functools

import jax
import jax.numpy as jnp
import numpy as np
from jax import lax
from jax.experimental import pallas as pl
from jax.experimental.pallas import tpu as pltpu
from jax.sharding import PartitionSpec as P

HEADS = 16
HD = 32
Q_LAT = 4
D = 512
CELLS = 72
TILES = CELLS // 8
PART = 40
EPS = 1e-05
BF = jnp.bfloat16
F32 = jnp.float32
EXP_SCALE = float(np.log2(np.e) / np.sqrt(HD))


MESH = pl.DeviceIdType.MESH
ORDERS = ((0, 1, 2), (1, 2, 0), (2, 0, 1))


class Place:
    def __init__(self):
        self.lev = lax.axis_index("lev")
        lat = lax.axis_index("lat")
        self.lat = lat
        self.core = lax.rem(lat, 2)
        xh = lax.rem(lat // 2, 2)
        self.pos = (xh * 2 + self.lev, lat // 16, lax.rem(lat // 4, 4))

    def device(self, axis=None, step=0, core=None):
        x, y, z = [lax.rem(p + step, 4) if a == axis else p for a, p in enumerate(self.pos)]
        c = self.core if core is None else core
        return (lax.rem(x, 2), ((y * 4 + z) * 2 + x // 2) * 2 + c)


def region(where, core):
    x, y, z = where
    full = slice(None)
    if x is None:
        xl, xh = full, full
    elif isinstance(x, tuple):
        xl, xh = full, x[1]
    else:
        xl, xh = lax.rem(x, 2), x // 2

    def line(v):
        if v is None:
            return full
        if isinstance(v, tuple):
            return pl.ds(2 * v[1], 2)
        return v

    return (xl, line(y), line(z), xh, core)


SLOTS = 20
EARLY = 256
WIDTHS = (1152, 768, 1152)
STEPS = (1, 3, 2)


class Gather:
    def __init__(self, place, bufs, send, recv):
        self.place, self.bufs, self.send, self.recv = place, bufs, send, recv

    def copy(self, p, slot, index, device):
        at = self.bufs[p].at[index]
        return pltpu.make_async_remote_copy(
            src_ref=at,
            dst_ref=at,
            send_sem=self.send.at[p, slot],
            recv_sem=self.recv.at[p, slot],
            device_id=device,
            device_id_type=MESH,
        )

    def index(self, p, block, phase, step, core, columns, half=None):
        order = ORDERS[p]
        where = [None, None, None]
        for k, axis in enumerate(order):
            if k == phase:
                if step is not None:
                    where[axis] = lax.rem(self.place.pos[axis] + step, 4)
            elif k > phase:
                where[axis] = self.place.pos[axis]
            elif k == 0 and half is not None:
                where[axis] = ("pair", half)
        at = region(where, core)
        return (slice(None) if block is None else block,) + at + (slice(None), columns)

    def link(self, p, b, slot, coming):
        c = self.place.core
        full, early, late = slice(None), slice(0, EARLY), slice(EARLY, WIDTHS[p])
        if b is None:
            phase, at, b = 0, slot, 0
        elif 15 <= slot <= 17:
            phase, at = 1 - b, 3 + b * SLOTS + slot
        elif slot < 3:
            phase, at = 1, 3 + b * SLOTS + slot
        else:
            phase, at = 2, 3 + b * SLOTS + slot
        axis = ORDERS[p][phase]
        if phase == 0 or slot < 6 or 15 <= slot <= 17:
            k = slot % 3
            to = STEPS[k]
            columns = full
            if phase == 2 or (b == 0 and phase == 1):
                columns = late if slot < 3 else early
            step = (4 - to) % 4 if coming else 0
            return self.copy(p, at, self.index(p, b, phase, step, c, columns), self.place.device(axis, to))
        if slot in (7, 8, 9, 10):
            way, later = (slot - 7) // 2, (slot - 7) % 2
            to = STEPS[way]
            step = (4 - to) if coming else 0
            return self.copy(p, at, self.index(p, b, 2, step, c, late, way ^ later), self.place.device(axis, to))
        if slot in (11, 12):
            to = STEPS[slot - 11]
            step = 2 if coming else 4 - to
            return self.copy(p, at, self.index(p, b, 2, step, c, late, slot - 11), self.place.device(axis, to))
        c = 1 - c if coming else c
        other = self.place.device(core=1 - self.place.core)
        if slot == 6:
            return self.copy(p, at, self.index(p, b, 2, None, c, early), other)
        step = {13: 0, 14: 2, 18: 3, 19: 1}[slot]
        return self.copy(p, at, self.index(p, b, 2, step, c, late), other)

    def start(self, b, slots):
        for slot in slots:
            for p in range(3):
                self.link(p, b, slot, False).start()

    def wait(self, b, slots):
        for p in range(3):
            for slot in slots:
                self.link(p, b, slot, True).wait_recv()

    def step(self, b, waits, sends):
        for p in range(3):
            for slot in waits:
                self.link(p, b, slot, True).wait_recv()
            for slot in sends:
                self.link(p, b, slot, False).start()

    def drain(self, b, slots):
        for p in range(3):
            for slot in slots:
                self.link(p, b, slot, False).wait_send()


def greet(place, more):
    barrier = pltpu.get_barrier_semaphore()
    peers = [place.device(axis, step) for axis in range(3) for step in (1, 2, 3)]
    peers.append(place.device(core=1 - place.core))
    peers += more
    for peer in peers:
        pl.semaphore_signal(barrier, inc=1, device_id=peer, device_id_type=MESH)
    return barrier, len(peers)


def dot(a, b, dims=((1,), (0,))):
    return lax.dot_general(a, b, (dims, ((), ())), preferred_element_type=F32)


def layer_norm(flat, gain):
    mean = jnp.mean(flat, -1, keepdims=True)
    centred = flat - mean
    var = jnp.mean(centred * centred, -1, keepdims=True)
    return (centred * lax.rsqrt(var + EPS) * gain).astype(BF)


def gelu(x):
    inner = x * (0.7978845608028654 + 0.035677408136300125 * x * x)
    half = 0.5 * x
    return half + half * jnp.tanh(inner)


def one_hot(rows, columns, pairs):
    out = np.zeros((rows, columns), np.float32)
    for i, j in pairs:
        out[i, j] = 1.0
    return out


def cells():
    for k in range(4):
        for r in range(6):
            for c in range(12):
                yield k, r, c


def quarter_row(k, r, c):
    return (((r // 3) * 2 + c // 6) * 2 + k // 2) * PART + (k % 2) * 18 + (r % 3) * 6 + c % 6


def row_orders():
    halves = np.stack(
        [
            one_hot(
                2 * CELLS,
                144,
                [
                    (side * CELLS + r * 12 + c, r * 24 + c + 12 * (lev ^ side))
                    for side in range(2)
                    for r in range(6)
                    for c in range(12)
                ],
            )
            for lev in range(2)
        ]
    )
    cut = one_hot(
        4 * PART,
        144,
        [
            (((r // 3) * 2 + c // 6) * PART + k * 18 + (r % 3) * 6 + c % 6, k * 72 + r * 12 + c)
            for k, r, c in cells()
            if k < 2
        ],
    )
    rolled = one_hot(
        288, 8 * PART, [(k * 72 + r * 12 + c, quarter_row((k + 1) % 4, r, c)) for k, r, c in cells()]
    )
    back = one_hot(
        288, 8 * PART, [(r * 48 + c * 4 + (k + 1) % 4, quarter_row(k, r, c)) for k, r, c in cells()]
    )
    return [a.astype(BF) for a in (halves, cut, rolled, back)]


def head_spread():
    rows = np.arange(Q_LAT * HEADS)
    return (np.arange(D)[None, :] // HD == rows[:, None] % HEADS).astype(BF)


def pick_head(shape, j):
    lane = lax.broadcasted_iota(jnp.int32, shape, 1)
    return (lane >= j * HD) & (lane < (j + 1) * HD)


def region_bias(ids):
    kinds = lax.broadcasted_iota(jnp.int32, (8, 144), 0)
    hot = (kinds == jnp.broadcast_to(ids, (8, 144))).astype(F32).astype(BF)
    bias = jnp.where(dot(hot, hot, ((0,), (0,))) > 0.5, 0.0, -1e30)
    return jnp.concatenate([bias] * 4, 1)


def attention(q, k, v, mask):
    parts = []
    for g in range(4):
        lanes = slice(g * 128, (g + 1) * 128)
        kg, vg, qg = k[:, lanes], v[:, lanes], q[:, lanes]
        heads = [pick_head((144, 128), j) for j in range(4)]
        qs = jnp.concatenate([jnp.where(h, qg, jnp.zeros_like(qg)) for h in heads], 0)
        score = dot(kg, qs, ((1,), (1,)))
        if mask is not None:
            score = score + mask
        top = jnp.max(score, 0, keepdims=True)
        weight = jnp.exp2((score - top) * EXP_SCALE)
        weight = (weight * (1.0 / jnp.sum(weight, 0, keepdims=True))).astype(BF)
        out = dot(weight, vg, ((0,), (0,)))
        ctx = jnp.zeros((144, 128), F32)
        for j, h in enumerate(heads):
            ctx = jnp.where(h, out[j * 144 : (j + 1) * 144], ctx)
        parts.append(ctx.astype(BF))
    return jnp.concatenate(parts, 1)


class Block:
    def __init__(self, b, bufs, gain_one, gain_two):
        self.b, self.bufs = b, bufs
        self.gain_one = gain_one[b : b + 1, :]
        self.gain_two = gain_two[b : b + 1, :]

    def tile(self, p, h, first, last):
        return self.bufs[p][self.b, h, :, :, :, :, :, first:last].reshape(D, last - first)

    def qkv(self, x):
        n1 = layer_norm(x, self.gain_one)
        return [
            jnp.concatenate([dot(n1, self.tile(p, h, 0, 256)).astype(BF) for h in range(2)], 1) for p in range(3)
        ]

    def window(self, qkv, w, regions=None):
        q, k, v = [part[w * 144 : (w + 1) * 144] for part in qkv]
        return attention(q, k, v, None if regions is None else regions[w])

    def mix(self, x, context):
        added = [dot(context, self.tile(1, h, 512, 768)) for h in range(2)]
        return (x + jnp.concatenate(added, 1)).astype(BF).astype(F32)

    def feed(self, mixed):
        b = self.b
        n2 = layer_norm(mixed, self.gain_two)
        sums = [0.0, 0.0]
        for h in range(2):
            up = [dot(n2, self.tile(0, h, 256, 1024)), dot(n2, self.tile(1, h, 256, 512))]
            hidden = jnp.concatenate([gelu(u).astype(BF) for u in up], 1)
            for side in range(2):

                def line(p, first, width):
                    part = self.bufs[p][b, side, 2 * h : 2 * h + 2, :, :, :, :, first : first + width]
                    return part.reshape(32, 8, width)

                lines = [jnp.concatenate([line(0, 1024, 128), line(2, 1024, 128)], 2)]
                lines += [line(2, 256 * i, 256) for i in range(1, 4)]
                wd = jnp.stack(lines, 1).reshape(1024, 256)
                sums[side] = sums[side] + dot(hidden, wd)
        return (mixed + jnp.concatenate(sums, 1)).astype(BF)


def moved(send_buf, recv_buf, sems, w, slot, peer, quarter):
    return pltpu.make_async_remote_copy(
        src_ref=send_buf.at[w, quarter],
        dst_ref=recv_buf.at[slot, w],
        send_sem=sems[0].at[slot, w],
        recv_sem=sems[1].at[slot, w],
        device_id=peer,
        device_id_type=MESH,
    )


def tiles_of(own, quarter, received):
    parts = [own[w, quarter].reshape(PART, D) for w in range(2)]
    return parts, [received[slot].reshape(2 * PART, D) for slot in range(3)]


def kernel(
    level_ids,
    level_table_h,
    latent_query_h,
    regions_h,
    gain_one_h,
    gain_two_h,
    tokens_h,
    halves_h,
    w_qkv_h,
    w_proj_h,
    w_up_h,
    w_down_h,
    w_query_h,
    w_kv_h,
    spread_h,
    w_attn_out_h,
    columns_h,
    cut_h,
    roll_rows_h,
    back_rows_h,
    out,
    level_table,
    latent_query,
    regions,
    gain_one,
    gain_two,
    tokens,
    halves,
    w_qkv,
    w_proj,
    w_up,
    w_down,
    w_query,
    w_kv,
    spread,
    w_attn_out,
    columns,
    cut,
    roll_rows,
    back_rows,
    ba,
    bb,
    bc,
    tok_own,
    tok_send,
    tok_recv,
    hs,
    hr,
    hs2,
    hr2,
    send,
    recv,
    tok_sem,
    hsem,
    hrsem,
    h2sem,
    h2rsem,
    load_sem,
):
    place = Place()
    lev, lat = place.lev, place.lat
    partner = (1 - lev, lat)
    ahead, behind = lax.rem(lat + 1, 64), lax.rem(lat + 63, 64)
    barrier, count = greet(place, [(lev, ahead), (lev, behind), (1 - lev, ahead), (1 - lev, behind)])
    pairs = (
        (w_qkv_h, w_qkv),
        (w_proj_h, w_proj),
        (w_up_h, w_up),
        (w_down_h, w_down),
        (level_table_h, level_table),
        (tokens_h, tokens),
        (halves_h, halves),
        (latent_query_h, latent_query),
        (w_query_h, w_query),
        (spread_h, spread),
        (w_kv_h, w_kv),
        (w_attn_out_h, w_attn_out),
        (gain_one_h, gain_one),
        (gain_two_h, gain_two),
        (regions_h, regions),
        (columns_h, columns),
        (cut_h, cut),
        (roll_rows_h, roll_rows),
        (back_rows_h, back_rows),
    )
    loads = [pltpu.make_async_copy(src, dst, load_sem.at[n]) for n, (src, dst) in enumerate(pairs)]
    for load in loads:
        load.start()

    def loaded(first, last):
        for load in loads[first:last]:
            load.wait()

    bufs = (ba, bb, bc)
    g = Gather(place, bufs, send, recv)
    first = lev == 0

    def half(array, start, width, apart):
        return jnp.where(first, array[:, start : start + width], array[:, start + apart : start + apart + width])

    loaded(0, 4)
    for blk in range(2):
        at = (blk,) + region(place.pos, place.core)
        qkv, up, down = w_qkv[blk], w_up[blk], half(w_down[blk], 0, 256, 256)
        lines = [down[8 * i : 8 * i + 8] for i in range(4)]
        ba[at] = jnp.concatenate([half(qkv, 0, 256, 256), half(up, 0, 768, 1024), lines[0][:, 0:128]], 1)
        bb[at] = jnp.concatenate(
            [half(qkv, 512, 256, 256), half(up, 768, 256, 1024), half(w_proj[blk], 0, 256, 256)], 1
        )
        bc[at] = jnp.concatenate([half(qkv, 1024, 256, 256)] + lines[1:] + [lines[0][:, 128:256]], 1)
    pl.semaphore_wait(barrier, count)

    g.start(None, (0, 1, 2))
    g.start(1, (15, 16, 17))
    loaded(4, 7)
    select = halves[lev]
    for slot in range(4):
        row = level_table[pl.ds(level_ids[slot], 1), :]
        summed = (tokens[slot].astype(F32).reshape(144, D) + row).astype(BF)
        both = dot(select, summed)
        tok_own[slot] = both[0:CELLS].reshape(TILES, 8, D).astype(BF)
        tok_send[slot] = both[CELLS : 2 * CELLS].reshape(TILES, 8, D).astype(BF)
    toks = [
        pltpu.make_async_remote_copy(
            src_ref=tok_send.at[pl.ds(2 * n, 2)],
            dst_ref=tok_recv.at[pl.ds(2 * n, 2)],
            send_sem=tok_sem.at[2 * n],
            recv_sem=tok_sem.at[2 * n + 1],
            device_id=partner,
            device_id_type=MESH,
        )
        for n in range(2)
    ]
    toks[0].start()

    loaded(7, 11)
    queries = dot(latent_query[...], w_query[...]).astype(BF).astype(F32)
    wide_q = jnp.concatenate(
        [jnp.broadcast_to(queries[q : q + 1], (HEADS, D)) for q in range(Q_LAT)], 0
    )
    query_block = (wide_q * spread[...].astype(F32)).astype(BF)

    def keys_values(ref):
        kv = dot(ref[...].reshape(4 * CELLS, D), w_kv[...]).astype(BF)
        score = dot(kv[:, 0:D], query_block, ((1,), (1,)))
        return score.reshape(4, CELLS, Q_LAT * HEADS), kv[:, D : 2 * D].astype(F32).reshape(4, CELLS, D)

    g.step(None, (0, 1, 2), ())
    g.start(0, (15, 16, 17, 0, 1, 2))
    toks[1].start()
    score_own, val_own = keys_values(tok_own)
    g.step(0, (15, 16, 17), (3, 4, 5))
    g.wait(0, (0, 1, 2))
    g.start(0, (7, 9, 8, 10, 13))
    g.wait(1, (15, 16, 17))
    g.start(1, (0, 1, 2))
    toks[0].wait_recv()
    toks[1].wait_recv()
    score_par, val_par = keys_values(tok_recv)
    top = jnp.maximum(jnp.max(score_own, 0), jnp.max(score_par, 0))
    w_own = jnp.exp2((score_own - top) * EXP_SCALE)
    w_par = jnp.exp2((score_par - top) * EXP_SCALE)
    inverse = 1.0 / (jnp.sum(w_own, 0) + jnp.sum(w_par, 0))
    w_own = (w_own * inverse).reshape(4 * CELLS, Q_LAT * HEADS).astype(BF)
    w_par = (w_par * inverse).reshape(4 * CELLS, Q_LAT * HEADS).astype(BF)
    attended = []
    line = lax.broadcasted_iota(jnp.int32, (Q_LAT * HEADS, D), 0)
    for q in range(Q_LAT):
        mine = (line >= q * HEADS) & (line < (q + 1) * HEADS)
        owner = jnp.where(mine, spread[...], jnp.zeros((Q_LAT * HEADS, D), BF))
        total = jnp.sum(dot(w_own, owner).reshape(4, CELLS, D) * val_own, 0)
        total = total + jnp.sum(dot(w_par, owner).reshape(4, CELLS, D) * val_par, 0)
        attended.append(total)
    attended = jnp.concatenate(attended, 0).astype(BF)
    base = jnp.concatenate([jnp.broadcast_to(queries[q : q + 1], (CELLS, D)) for q in range(Q_LAT)], 0)
    loaded(11, 16)
    x = (dot(attended, w_attn_out[...]) + base).astype(BF).astype(F32)
    g.step(0, (3, 4, 5), (6,))
    g.wait(0, (6,))

    block = Block(0, bufs, gain_one, gain_two)
    g.step(0, (7, 9), (11, 12))
    qkv = block.qkv(x)
    context = [block.window(qkv, 0)]
    g.step(0, (8, 10), (18, 19))
    g.step(1, (0, 1, 2), (3, 4, 5))
    g.start(1, (7, 9, 8, 10, 13))
    context.append(block.window(qkv, 1))
    g.step(0, (11, 12), (14,))
    g.drain(None, (0, 1, 2))
    g.drain(0, (0, 1, 2, 3, 4, 5, 6, 15, 16, 17))
    placed = dot(regions[0].astype(F32).astype(BF), columns[0])
    for r in range(1, 6):
        placed = placed + dot(regions[r].astype(F32).astype(BF), columns[r])
    ids = placed.astype(jnp.int32)
    labels = [jnp.concatenate([ids[2 * w : 2 * w + 1], ids[2 * w + 1 : 2 * w + 2]], 1) for w in range(2)]
    labels = [region_bias(label) for label in labels]
    loaded(16, 19)
    g.wait(0, (13, 18, 19, 14))
    sems = (hsem, hrsem)
    sent = []
    for w in range(2):
        mixed = block.mix(x[w * 144 : (w + 1) * 144], context[w])
        plain = block.feed(mixed)
        hs[w] = dot(cut[...], plain).reshape(4, PART // 8, 8, D).astype(BF)
        now = [
            moved(hs, hr, sems, w, 1, (lev, behind), 1),
            moved(hs, hr, sems, w, 0, partner, 2),
            moved(hs, hr, sems, w, 2, (1 - lev, behind), 0),
        ]
        for copy in now:
            copy.start()
        sent += now
    g.step(1, (7, 9), (11, 12))
    g.step(1, (3, 4, 5), (6,))
    g.step(1, (8, 10), (18, 19))
    for copy in sent:
        copy.wait_recv()
    own, others = tiles_of(hs, 3, hr)
    tiles = jnp.concatenate(own + others, 0)
    x = dot(roll_rows[...], tiles)
    g.wait(1, (6,))

    block = Block(1, bufs, gain_one, gain_two)
    qkv = block.qkv(x)
    context = [block.window(qkv, 0, labels)]
    g.step(1, (11, 12), (14,))
    context.append(block.window(qkv, 1, labels))
    g.wait(1, (13, 18, 19, 14))
    sems = (h2sem, h2rsem)
    back = []
    for w in range(2):
        mixed = block.mix(x[w * 144 : (w + 1) * 144], context[w])
        shifted = block.feed(mixed)
        hs2[w] = dot(cut[...], shifted).reshape(4, PART // 8, 8, D).astype(BF)
        now = [
            moved(hs2, hr2, sems, w, 1, (lev, ahead), 2),
            moved(hs2, hr2, sems, w, 0, partner, 1),
            moved(hs2, hr2, sems, w, 2, (1 - lev, ahead), 3),
        ]
        for copy in now:
            copy.start()
        back += now
    for tok in toks:
        tok.wait_send()
    g.drain(0, (7, 8, 9, 10, 11, 12, 13, 14, 18, 19))
    g.drain(1, range(SLOTS))
    for copy in sent:
        copy.wait_send()
    for copy in back:
        copy.wait_recv()
    own, others = tiles_of(hs2, 0, hr2)
    tiles = jnp.concatenate(others[::-1] + own, 0)
    out[...] = dot(back_rows[...], tiles).astype(BF)
    for copy in back:
        copy.wait_send()


def local(
    tokens,
    level_ids,
    level_table,
    latent_query,
    w_query,
    w_kv,
    w_attn_out,
    regions,
    gain_one,
    gain_two,
    w_qkv,
    w_proj,
    w_up,
    w_down,
):
    place_row = np.stack([one_hot(12, 72, [(c, r * 12 + c) for c in range(12)]) for r in range(6)])
    halves, cut, roll_rows, back_rows = [jnp.asarray(a) for a in row_orders()]
    operands = (
        level_table,
        latent_query,
        jnp.transpose(regions, (0, 2, 1)),
        gain_one,
        gain_two,
        tokens,
        halves,
        w_qkv,
        w_proj,
        w_up,
        w_down,
        w_query,
        w_kv,
        jnp.asarray(head_spread()),
        w_attn_out,
        jnp.asarray(place_row.astype(BF)),
        cut,
        roll_rows,
        back_rows,
    )
    buf = pltpu.VMEM
    dma = pltpu.SemaphoreType.DMA
    flat = pl.pallas_call(
        kernel,
        out_shape=jax.ShapeDtypeStruct((288, D), BF),
        in_specs=[pl.BlockSpec(memory_space=pltpu.SMEM)]
        + [pl.BlockSpec(memory_space=pl.ANY)] * len(operands),
        out_specs=pl.BlockSpec(memory_space=pltpu.VMEM),
        scratch_shapes=[buf(a.shape, a.dtype) for a in operands]
        + [buf((2, 2, 4, 4, 2, 2, 8, width), BF) for width in WIDTHS]
        + [buf((4, TILES, 8, D), BF)] * 3
        + [buf(lead + (PART // 8, 8, D), BF) for lead in ((2, 4), (3, 2)) * 2]
        + [
            dma((3, 3 + 2 * SLOTS)),
            dma((3, 3 + 2 * SLOTS)),
            dma((4,)),
            dma((3, 2)),
            dma((3, 2)),
            dma((3, 2)),
            dma((3, 2)),
            dma((len(operands),)),
        ],
        compiler_params=pltpu.CompilerParams(
            collective_id=0, has_side_effects=True, vmem_limit_bytes=56 << 20
        ),
        name="encode_and_blocks",
    )(level_ids, *operands)
    return flat.reshape(6, 12, Q_LAT, D)


def solution(mesh):
    in_specs = (
        P("lev", "lat", None, None),
        P("lev"),
        P(),
        P(),
        P(),
        P(),
        P(),
        P("lat", "lev", None),
        P(),
        P(),
        P(None, "lat", None),
        P(None, "lat", None),
        P(None, "lat", None),
        P(None, "lat", None),
    )
    out_specs = P("lat", "lev", None, None)
    return jax.shard_map(local, mesh=mesh, in_specs=in_specs, out_specs=out_specs, check_vma=False)
```

```python
import functools

import jax
import jax.numpy as jnp
import numpy as np
from jax import lax
from jax.experimental import pallas as pl
from jax.experimental.pallas import tpu as pltpu
from jax.sharding import PartitionSpec as P

HEADS = 16
HD = 32
Q_LAT = 4
D = 512
CELLS = 72
TILES = CELLS // 8
PART = 40
EPS = 1e-05
BF = jnp.bfloat16
F32 = jnp.float32
EXP_SCALE = float(np.log2(np.e) / np.sqrt(HD))


MESH = pl.DeviceIdType.MESH
ORDERS = ((0, 1, 2), (1, 2, 0), (2, 0, 1))


class Place:
    def __init__(self):
        self.lev = lax.axis_index("lev")
        lat = lax.axis_index("lat")
        self.lat = lat
        self.core = lax.rem(lat, 2)
        xh = lax.rem(lat // 2, 2)
        self.pos = (xh * 2 + self.lev, lat // 16, lax.rem(lat // 4, 4))

    def device(self, axis=None, step=0, core=None):
        x, y, z = [lax.rem(p + step, 4) if a == axis else p for a, p in enumerate(self.pos)]
        c = self.core if core is None else core
        return (lax.rem(x, 2), ((y * 4 + z) * 2 + x // 2) * 2 + c)


def region(where, core):
    x, y, z = where
    full = slice(None)
    if x is None:
        xl, xh = full, full
    elif isinstance(x, tuple):
        xl, xh = full, x[1]
    else:
        xl, xh = lax.rem(x, 2), x // 2

    def line(v):
        if v is None:
            return full
        if isinstance(v, tuple):
            return pl.ds(2 * v[1], 2)
        return v

    return (xl, line(y), line(z), xh, core)


SLOTS = 20
EARLY = 256
WIDTHS = (1152, 768, 1152)
STEPS = (1, 3, 2)


class Gather:
    def __init__(self, place, bufs, send, recv):
        self.place, self.bufs, self.send, self.recv = place, bufs, send, recv

    def copy(self, p, slot, index, device):
        at = self.bufs[p].at[index]
        return pltpu.make_async_remote_copy(
            src_ref=at,
            dst_ref=at,
            send_sem=self.send.at[p, slot],
            recv_sem=self.recv.at[p, slot],
            device_id=device,
            device_id_type=MESH,
        )

    def index(self, p, block, phase, step, core, columns, half=None):
        order = ORDERS[p]
        where = [None, None, None]
        for k, axis in enumerate(order):
            if k == phase:
                if step is not None:
                    where[axis] = lax.rem(self.place.pos[axis] + step, 4)
            elif k > phase:
                where[axis] = self.place.pos[axis]
            elif k == 0 and half is not None:
                where[axis] = ("pair", half)
        at = region(where, core)
        return (slice(None) if block is None else block,) + at + (slice(None), columns)

    def link(self, p, b, slot, coming):
        c = self.place.core
        full, early, late = slice(None), slice(0, EARLY), slice(EARLY, WIDTHS[p])
        if b is None:
            phase, at, b = 0, slot, 0
        elif 15 <= slot <= 17:
            phase, at = 1 - b, 3 + b * SLOTS + slot
        elif slot < 3:
            phase, at = 1, 3 + b * SLOTS + slot
        else:
            phase, at = 2, 3 + b * SLOTS + slot
        axis = ORDERS[p][phase]
        if phase == 0 or slot < 6 or 15 <= slot <= 17:
            k = slot % 3
            to = STEPS[k]
            columns = full
            if phase == 2 or (b == 0 and phase == 1):
                columns = late if slot < 3 else early
            step = (4 - to) % 4 if coming else 0
            return self.copy(p, at, self.index(p, b, phase, step, c, columns), self.place.device(axis, to))
        if slot in (7, 8, 9, 10):
            way, later = (slot - 7) // 2, (slot - 7) % 2
            to = STEPS[way]
            step = (4 - to) if coming else 0
            return self.copy(p, at, self.index(p, b, 2, step, c, late, way ^ later), self.place.device(axis, to))
        if slot in (11, 12):
            to = STEPS[slot - 11]
            step = 2 if coming else 4 - to
            return self.copy(p, at, self.index(p, b, 2, step, c, late, slot - 11), self.place.device(axis, to))
        c = 1 - c if coming else c
        other = self.place.device(core=1 - self.place.core)
        if slot == 6:
            return self.copy(p, at, self.index(p, b, 2, None, c, early), other)
        step = {13: 0, 14: 2, 18: 3, 19: 1}[slot]
        return self.copy(p, at, self.index(p, b, 2, step, c, late), other)

    def start(self, b, slots):
        for slot in slots:
            for p in range(3):
                self.link(p, b, slot, False).start()

    def wait(self, b, slots):
        for p in range(3):
            for slot in slots:
                self.link(p, b, slot, True).wait_recv()

    def step(self, b, waits, sends):
        for p in range(3):
            for slot in waits:
                self.link(p, b, slot, True).wait_recv()
            for slot in sends:
                self.link(p, b, slot, False).start()

    def drain(self, b, slots):
        for p in range(3):
            for slot in slots:
                self.link(p, b, slot, False).wait_send()


def greet(place, more):
    barrier = pltpu.get_barrier_semaphore()
    peers = [place.device(axis, step) for axis in range(3) for step in (1, 2, 3)]
    peers.append(place.device(core=1 - place.core))
    peers += more
    for peer in peers:
        pl.semaphore_signal(barrier, inc=1, device_id=peer, device_id_type=MESH)
    return barrier, len(peers)


def dot(a, b, dims=((1,), (0,))):
    return lax.dot_general(a, b, (dims, ((), ())), preferred_element_type=F32)


def layer_norm(flat, gain):
    mean = jnp.mean(flat, -1, keepdims=True)
    centred = flat - mean
    var = jnp.mean(centred * centred, -1, keepdims=True)
    return (centred * lax.rsqrt(var + EPS) * gain).astype(BF)


def gelu(x):
    inner = x * (0.7978845608028654 + 0.035677408136300125 * x * x)
    half = 0.5 * x
    return half + half * jnp.tanh(inner)


def one_hot(rows, columns, pairs):
    out = np.zeros((rows, columns), np.float32)
    for i, j in pairs:
        out[i, j] = 1.0
    return out


def cells():
    for k in range(4):
        for r in range(6):
            for c in range(12):
                yield k, r, c


def quarter_row(k, r, c):
    return (((r // 3) * 2 + c // 6) * 2 + k // 2) * PART + (k % 2) * 18 + (r % 3) * 6 + c % 6


def row_orders():
    halves = np.stack(
        [
            one_hot(
                2 * CELLS,
                144,
                [
                    (side * CELLS + r * 12 + c, r * 24 + c + 12 * (lev ^ side))
                    for side in range(2)
                    for r in range(6)
                    for c in range(12)
                ],
            )
            for lev in range(2)
        ]
    )
    cut = one_hot(
        4 * PART,
        144,
        [
            (((r // 3) * 2 + c // 6) * PART + k * 18 + (r % 3) * 6 + c % 6, k * 72 + r * 12 + c)
            for k, r, c in cells()
            if k < 2
        ],
    )
    rolled = one_hot(
        288, 8 * PART, [(k * 72 + r * 12 + c, quarter_row((k + 1) % 4, r, c)) for k, r, c in cells()]
    )
    back = one_hot(
        288, 8 * PART, [(r * 48 + c * 4 + (k + 1) % 4, quarter_row(k, r, c)) for k, r, c in cells()]
    )
    return [a.astype(BF) for a in (halves, cut, rolled, back)]


def head_spread():
    rows = np.arange(Q_LAT * HEADS)
    return (np.arange(D)[None, :] // HD == rows[:, None] % HEADS).astype(BF)


def pick_head(shape, j):
    lane = lax.broadcasted_iota(jnp.int32, shape, 1)
    return (lane >= j * HD) & (lane < (j + 1) * HD)


def region_bias(ids):
    kinds = lax.broadcasted_iota(jnp.int32, (8, 144), 0)
    hot = (kinds == jnp.broadcast_to(ids, (8, 144))).astype(F32).astype(BF)
    bias = jnp.where(dot(hot, hot, ((0,), (0,))) > 0.5, 0.0, -1e30)
    return jnp.concatenate([bias] * 4, 1)


def attention(q, k, v, mask):
    parts = []
    for g in range(4):
        lanes = slice(g * 128, (g + 1) * 128)
        kg, vg, qg = k[:, lanes], v[:, lanes], q[:, lanes]
        heads = [pick_head((144, 128), j) for j in range(4)]
        qs = jnp.concatenate([jnp.where(h, qg, jnp.zeros_like(qg)) for h in heads], 0)
        score = dot(kg, qs, ((1,), (1,)))
        if mask is not None:
            score = score + mask
        top = jnp.max(score, 0, keepdims=True)
        weight = jnp.exp2((score - top) * EXP_SCALE)
        weight = (weight * (1.0 / jnp.sum(weight, 0, keepdims=True))).astype(BF)
        out = dot(weight, vg, ((0,), (0,)))
        ctx = jnp.zeros((144, 128), F32)
        for j, h in enumerate(heads):
            ctx = jnp.where(h, out[j * 144 : (j + 1) * 144], ctx)
        parts.append(ctx.astype(BF))
    return jnp.concatenate(parts, 1)


class Block:
    def __init__(self, b, bufs, gain_one, gain_two):
        self.b, self.bufs = b, bufs
        self.gain_one = gain_one[b : b + 1, :]
        self.gain_two = gain_two[b : b + 1, :]

    def tile(self, p, h, first, last):
        return self.bufs[p][self.b, h, :, :, :, :, :, first:last].reshape(D, last - first)

    def qkv(self, x):
        n1 = layer_norm(x, self.gain_one)
        return [
            jnp.concatenate([dot(n1, self.tile(p, h, 0, 256)).astype(BF) for h in range(2)], 1) for p in range(3)
        ]

    def window(self, qkv, w, regions=None):
        q, k, v = [part[w * 144 : (w + 1) * 144] for part in qkv]
        return attention(q, k, v, None if regions is None else regions[w])

    def mix(self, x, context):
        added = [dot(context, self.tile(1, h, 512, 768)) for h in range(2)]
        return (x + jnp.concatenate(added, 1)).astype(BF).astype(F32)

    def feed(self, mixed):
        b = self.b
        n2 = layer_norm(mixed, self.gain_two)
        sums = [0.0, 0.0]
        for h in range(2):
            up = [dot(n2, self.tile(0, h, 256, 1024)), dot(n2, self.tile(1, h, 256, 512))]
            hidden = jnp.concatenate([gelu(u).astype(BF) for u in up], 1)
            for side in range(2):

                def line(p, first, width):
                    part = self.bufs[p][b, side, 2 * h : 2 * h + 2, :, :, :, :, first : first + width]
                    return part.reshape(32, 8, width)

                lines = [jnp.concatenate([line(0, 1024, 128), line(2, 1024, 128)], 2)]
                lines += [line(2, 256 * i, 256) for i in range(1, 4)]
                wd = jnp.stack(lines, 1).reshape(1024, 256)
                sums[side] = sums[side] + dot(hidden, wd)
        return (mixed + jnp.concatenate(sums, 1)).astype(BF)


def moved(send_buf, recv_buf, sems, w, slot, peer, quarter):
    return pltpu.make_async_remote_copy(
        src_ref=send_buf.at[w, quarter],
        dst_ref=recv_buf.at[slot, w],
        send_sem=sems[0].at[slot, w],
        recv_sem=sems[1].at[slot, w],
        device_id=peer,
        device_id_type=MESH,
    )


def tiles_of(own, quarter, received):
    parts = [own[w, quarter].reshape(PART, D) for w in range(2)]
    return parts, [received[slot].reshape(2 * PART, D) for slot in range(3)]


def kernel(
    level_ids,
    level_table_h,
    latent_query_h,
    regions_h,
    gain_one_h,
    gain_two_h,
    tokens_h,
    halves_h,
    w_qkv_h,
    w_proj_h,
    w_up_h,
    w_down_h,
    w_query_h,
    w_kv_h,
    spread_h,
    w_attn_out_h,
    columns_h,
    cut_h,
    roll_rows_h,
    out,
    level_table,
    latent_query,
    regions,
    gain_one,
    gain_two,
    tokens,
    halves,
    w_qkv,
    w_proj,
    w_up,
    w_down,
    w_query,
    w_kv,
    spread,
    w_attn_out,
    columns,
    cut,
    roll_rows,
    ba,
    bb,
    bc,
    tok_own,
    tok_send,
    tok_recv,
    hs,
    hr,
    hs2,
    hr2,
    send,
    recv,
    tok_sem,
    hsem,
    hrsem,
    h2sem,
    h2rsem,
    load_sem,
):
    place = Place()
    lev, lat = place.lev, place.lat
    partner = (1 - lev, lat)
    ahead, behind = lax.rem(lat + 1, 64), lax.rem(lat + 63, 64)
    barrier, count = greet(place, [(lev, ahead), (lev, behind), (1 - lev, ahead), (1 - lev, behind)])
    pairs = (
        (w_qkv_h, w_qkv),
        (w_proj_h, w_proj),
        (w_up_h, w_up),
        (w_down_h, w_down),
        (level_table_h, level_table),
        (tokens_h, tokens),
        (halves_h, halves),
        (latent_query_h, latent_query),
        (w_query_h, w_query),
        (spread_h, spread),
        (w_kv_h, w_kv),
        (w_attn_out_h, w_attn_out),
        (gain_one_h, gain_one),
        (gain_two_h, gain_two),
        (regions_h, regions),
        (columns_h, columns),
        (cut_h, cut),
        (roll_rows_h, roll_rows),
    )
    loads = [pltpu.make_async_copy(src, dst, load_sem.at[n]) for n, (src, dst) in enumerate(pairs)]
    for load in loads:
        load.start()

    def loaded(first, last):
        for load in loads[first:last]:
            load.wait()

    bufs = (ba, bb, bc)
    g = Gather(place, bufs, send, recv)
    first = lev == 0

    def half(array, start, width, apart):
        return jnp.where(first, array[:, start : start + width], array[:, start + apart : start + apart + width])

    loaded(0, 4)
    for blk in range(2):
        at = (blk,) + region(place.pos, place.core)
        qkv, up, down = w_qkv[blk], w_up[blk], half(w_down[blk], 0, 256, 256)
        lines = [down[8 * i : 8 * i + 8] for i in range(4)]
        ba[at] = jnp.concatenate([half(qkv, 0, 256, 256), half(up, 0, 768, 1024), lines[0][:, 0:128]], 1)
        bb[at] = jnp.concatenate(
            [half(qkv, 512, 256, 256), half(up, 768, 256, 1024), half(w_proj[blk], 0, 256, 256)], 1
        )
        bc[at] = jnp.concatenate([half(qkv, 1024, 256, 256)] + lines[1:] + [lines[0][:, 128:256]], 1)
    pl.semaphore_wait(barrier, count)

    g.start(None, (0, 1, 2))
    g.start(1, (15, 16, 17))
    loaded(4, 7)
    select = halves[lev]
    for slot in range(4):
        row = level_table[pl.ds(level_ids[slot], 1), :]
        summed = (tokens[slot].astype(F32).reshape(144, D) + row).astype(BF)
        both = dot(select, summed)
        tok_own[slot] = both[0:CELLS].reshape(TILES, 8, D).astype(BF)
        tok_send[slot] = both[CELLS : 2 * CELLS].reshape(TILES, 8, D).astype(BF)
    toks = [
        pltpu.make_async_remote_copy(
            src_ref=tok_send.at[pl.ds(2 * n, 2)],
            dst_ref=tok_recv.at[pl.ds(2 * n, 2)],
            send_sem=tok_sem.at[2 * n],
            recv_sem=tok_sem.at[2 * n + 1],
            device_id=partner,
            device_id_type=MESH,
        )
        for n in range(2)
    ]
    toks[0].start()

    loaded(7, 11)
    queries = dot(latent_query[...], w_query[...]).astype(BF).astype(F32)
    wide_q = jnp.concatenate(
        [jnp.broadcast_to(queries[q : q + 1], (HEADS, D)) for q in range(Q_LAT)], 0
    )
    query_block = (wide_q * spread[...].astype(F32)).astype(BF)

    def keys_values(ref):
        kv = dot(ref[...].reshape(4 * CELLS, D), w_kv[...]).astype(BF)
        score = dot(kv[:, 0:D], query_block, ((1,), (1,)))
        return score.reshape(4, CELLS, Q_LAT * HEADS), kv[:, D : 2 * D].astype(F32).reshape(4, CELLS, D)

    g.step(None, (0, 1, 2), ())
    g.start(0, (15, 16, 17, 0, 1, 2))
    toks[1].start()
    score_own, val_own = keys_values(tok_own)
    g.step(0, (15, 16, 17), (3, 4, 5))
    g.wait(0, (0, 1, 2))
    g.start(0, (7, 9, 8, 10, 13))
    g.wait(1, (15, 16, 17))
    g.start(1, (0, 1, 2))
    toks[0].wait_recv()
    toks[1].wait_recv()
    score_par, val_par = keys_values(tok_recv)
    top = jnp.maximum(jnp.max(score_own, 0), jnp.max(score_par, 0))
    w_own = jnp.exp2((score_own - top) * EXP_SCALE)
    w_par = jnp.exp2((score_par - top) * EXP_SCALE)
    inverse = 1.0 / (jnp.sum(w_own, 0) + jnp.sum(w_par, 0))
    w_own = (w_own * inverse).reshape(4 * CELLS, Q_LAT * HEADS).astype(BF)
    w_par = (w_par * inverse).reshape(4 * CELLS, Q_LAT * HEADS).astype(BF)
    attended = []
    line = lax.broadcasted_iota(jnp.int32, (Q_LAT * HEADS, D), 0)
    for q in range(Q_LAT):
        mine = (line >= q * HEADS) & (line < (q + 1) * HEADS)
        owner = jnp.where(mine, spread[...], jnp.zeros((Q_LAT * HEADS, D), BF))
        total = jnp.sum(dot(w_own, owner).reshape(4, CELLS, D) * val_own, 0)
        total = total + jnp.sum(dot(w_par, owner).reshape(4, CELLS, D) * val_par, 0)
        attended.append(total)
    attended = jnp.concatenate(attended, 0).astype(BF)
    base = jnp.concatenate([jnp.broadcast_to(queries[q : q + 1], (CELLS, D)) for q in range(Q_LAT)], 0)
    loaded(11, 16)
    x = (dot(attended, w_attn_out[...]) + base).astype(BF).astype(F32)
    g.step(0, (3, 4, 5), (6,))
    g.wait(0, (6,))

    block = Block(0, bufs, gain_one, gain_two)
    g.step(0, (7, 9), (11, 12))
    qkv = block.qkv(x)
    context = [block.window(qkv, 0)]
    g.step(0, (8, 10), (18, 19))
    g.step(1, (0, 1, 2), (3, 4, 5))
    g.start(1, (7, 9, 8, 10, 13))
    context.append(block.window(qkv, 1))
    g.step(0, (11, 12), (14,))
    g.drain(None, (0, 1, 2))
    g.drain(0, (0, 1, 2, 3, 4, 5, 6, 15, 16, 17))
    placed = dot(regions[0].astype(F32).astype(BF), columns[0])
    for r in range(1, 6):
        placed = placed + dot(regions[r].astype(F32).astype(BF), columns[r])
    ids = placed.astype(jnp.int32)
    labels = [jnp.concatenate([ids[2 * w : 2 * w + 1], ids[2 * w + 1 : 2 * w + 2]], 1) for w in range(2)]
    labels = [region_bias(label) for label in labels]
    loaded(16, 18)
    g.wait(0, (13, 18, 19, 14))
    sems = (hsem, hrsem)
    sent = []
    for w in range(2):
        mixed = block.mix(x[w * 144 : (w + 1) * 144], context[w])
        plain = block.feed(mixed)
        hs[w] = dot(cut[...], plain).reshape(4, PART // 8, 8, D).astype(BF)
        now = [
            moved(hs, hr, sems, w, 1, (lev, behind), 1),
            moved(hs, hr, sems, w, 0, partner, 2),
            moved(hs, hr, sems, w, 2, (1 - lev, behind), 0),
        ]
        for copy in now:
            copy.start()
        sent += now
    g.step(1, (7, 9), (11, 12))
    g.step(1, (3, 4, 5), (6,))
    for copy in sent:
        copy.wait_recv()
    own, others = tiles_of(hs, 3, hr)
    tiles = jnp.concatenate(own + others, 0)
    x = dot(roll_rows[...], tiles)
    g.wait(1, (6,))

    block = Block(1, bufs, gain_one, gain_two)
    qkv = block.qkv(x)
    g.step(1, (8, 10), (18, 19))
    context = [block.window(qkv, 0, labels)]
    g.step(1, (11, 12), (14,))
    context.append(block.window(qkv, 1, labels))
    g.wait(1, (13, 18, 19, 14))
    sems = (h2sem, h2rsem)
    back = []
    for w in range(2):
        mixed = block.mix(x[w * 144 : (w + 1) * 144], context[w])
        shifted = block.feed(mixed)
        hs2[w] = dot(cut[...], shifted).reshape(4, PART // 8, 8, D).astype(BF)
        now = [
            moved(hs2, hr2, sems, w, 1, (lev, ahead), 2),
            moved(hs2, hr2, sems, w, 0, partner, 1),
            moved(hs2, hr2, sems, w, 2, (1 - lev, ahead), 3),
        ]
        for copy in now:
            copy.start()
        back += now
    for tok in toks:
        tok.wait_send()
    g.drain(0, (7, 8, 9, 10, 11, 12, 13, 14, 18, 19))
    g.drain(1, range(SLOTS))
    for copy in sent:
        copy.wait_send()
    for copy in back:
        copy.wait_recv()
    own, others = tiles_of(hs2, 0, hr2)
    out[...] = jnp.concatenate(others[::-1] + own, 0)
    for copy in back:
        copy.wait_send()


def in_order(order, tiles, out):
    out[...] = dot(order[...], tiles[...]).reshape(CELLS, Q_LAT, D).astype(BF)


def local(
    tokens,
    level_ids,
    level_table,
    latent_query,
    w_query,
    w_kv,
    w_attn_out,
    regions,
    gain_one,
    gain_two,
    w_qkv,
    w_proj,
    w_up,
    w_down,
):
    place_row = np.stack([one_hot(12, 72, [(c, r * 12 + c) for c in range(12)]) for r in range(6)])
    halves, cut, roll_rows, back_rows = [jnp.asarray(a) for a in row_orders()]
    operands = (
        level_table,
        latent_query,
        jnp.transpose(regions, (0, 2, 1)),
        gain_one,
        gain_two,
        tokens,
        halves,
        w_qkv,
        w_proj,
        w_up,
        w_down,
        w_query,
        w_kv,
        jnp.asarray(head_spread()),
        w_attn_out,
        jnp.asarray(place_row.astype(BF)),
        cut,
        roll_rows,
    )
    buf = pltpu.VMEM
    dma = pltpu.SemaphoreType.DMA
    flat = pl.pallas_call(
        kernel,
        out_shape=jax.ShapeDtypeStruct((8 * PART, D), BF),
        in_specs=[pl.BlockSpec(memory_space=pltpu.SMEM)]
        + [pl.BlockSpec(memory_space=pl.ANY)] * len(operands),
        out_specs=pl.BlockSpec(memory_space=pltpu.VMEM),
        scratch_shapes=[buf(a.shape, a.dtype) for a in operands]
        + [buf((2, 2, 4, 4, 2, 2, 8, width), BF) for width in WIDTHS]
        + [buf((4, TILES, 8, D), BF)] * 3
        + [buf(lead + (PART // 8, 8, D), BF) for lead in ((2, 4), (3, 2)) * 2]
        + [
            dma((3, 3 + 2 * SLOTS)),
            dma((3, 3 + 2 * SLOTS)),
            dma((4,)),
            dma((3, 2)),
            dma((3, 2)),
            dma((3, 2)),
            dma((3, 2)),
            dma((len(operands),)),
        ],
        compiler_params=pltpu.CompilerParams(
            collective_id=0, has_side_effects=True, vmem_limit_bytes=56 << 20
        ),
        name="encode_and_blocks",
    )(level_ids, *operands)
    vmem = pl.BlockSpec(memory_space=pltpu.VMEM)
    flat = pl.pallas_call(
        in_order,
        out_shape=jax.ShapeDtypeStruct((CELLS, Q_LAT, D), BF),
        in_specs=[vmem, vmem],
        out_specs=vmem,
        name="final_order",
    )(back_rows, flat)
    return flat.reshape(6, 12, Q_LAT, D)


def solution(mesh):
    in_specs = (
        P("lev", "lat", None, None),
        P("lev"),
        P(),
        P(),
        P(),
        P(),
        P(),
        P("lat", "lev", None),
        P(),
        P(),
        P(None, "lat", None),
        P(None, "lat", None),
        P(None, "lat", None),
        P(None, "lat", None),
    )
    out_specs = P("lat", "lev", None, None)
    return jax.shard_map(local, mesh=mesh, in_specs=in_specs, out_specs=out_specs, check_vma=False)
```
